128 devices in a mesh: section: 2 (over core), sht: 16 (over z, x), dp: 4 (over y).
Axes of the slice: x: 4, y: 4, z: 4, core: 2. Of those that a mesh axis runs over, the one named last changes fastest.
Arguments:
- fields_in: bfloat16 [32, 64, 128, 256], P('dp', 'sht'), may hold values from -6 to 6
- cotangent: bfloat16 [32, 64, 128, 256], P('dp', 'sht'), may hold values from -6 to 6
- weights: bfloat16 [2, 64, 256, 256], P('section'), may hold values from -0.375 to 0.375
Outputs:
- section_ends: bfloat16 [2, 32, 64, 128, 256], P('section', 'dp', 'sht')
- weight_grads: float32 [2, 64, 256, 256], P('section', ('sht', 'dp'))
The draws below stay inside these ranges and needn't reach their ends.
All inputs are finite; a program needn't handle non-finite values.
Results may differ from the reference program's by a relative error of at most 0.023.
Values may be sent and summed in bfloat16 or wider, within the bound.
No kernel may reach another device: no remote copies, remote signals or barrier semaphores. Data moves between devices by JAX's collectives and lax.ppermute only.
A program may use at most 192 MiB of HBM per device.

```python
import math
import jax
import jax.numpy as jnp
import numpy as np
from jax import lax

DEGREES = 64
CHANNELS = 256
LONGITUDES = 128
BATCH = 32


def block_levels(own_key, dims, split, least, largest):
    def one(axis_at, blocks):
        heights = jax.random.uniform(jax.random.fold_in(jax.random.fold_in(own_key, 6), axis_at), (blocks,), jnp.float32, least / len(split), largest / len(split))
        return jnp.repeat(jnp.exp(heights), dims[axis_at] // blocks).reshape((-1,) + (1,) * (len(dims) - axis_at - 1))

    gain = one(*split[0])
    for cut in split[1:]:
        gain = gain * one(*cut)
    return gain


def noise(rng, shape, deviation, bound, cuts=(), kind=jnp.bfloat16):
    array = jax.random.normal(rng, shape, jnp.float32) * deviation
    if len(cuts) > 0:
        array = block_levels(rng, shape, cuts, -0.22, 0.18) * array
    return jnp.clip(array, min=-bound, max=bound).astype(kind)


def setup_inputs(seed: int = 0) -> dict:
    splits = jax.random.split(jax.random.key(seed), 4)
    fields_in = noise(splits[0], (BATCH, DEGREES, LONGITUDES, CHANNELS), 1.0, 6.0, ((0, 4), (1, 16)))
    cotangent = noise(splits[1], (BATCH, DEGREES, LONGITUDES, CHANNELS), 1.0, 6.0, ((0, 4), (1, 16)))
    weights = noise(splits[2], (2, DEGREES, CHANNELS, CHANNELS), CHANNELS ** -0.5, 0.375, ((0, 2),))
    return dict(fields_in=fields_in, cotangent=cotangent, weights=weights)


def gauss_nodes(resolution):
    counter = np.arange(resolution) * 1.0
    guesses = np.cos(math.pi * (counter + 0.75) / (resolution + 0.5))
    for sweep in range(100):
        current = np.ones(resolution)
        previous = np.zeros(resolution)
        for degree in range(1, resolution + 1):
            following = ((2.0 * degree - 1.0) * guesses * current - (degree - 1.0) * previous) / degree
            previous = current
            current = following
        slope_val = resolution * (guesses * current - previous) / (guesses * guesses - 1.0)
        guesses = guesses - current / slope_val
    current = np.ones(resolution)
    previous = np.zeros(resolution)
    for degree in range(1, resolution + 1):
        following = ((2.0 * degree - 1.0) * guesses * current - (degree - 1.0) * previous) / degree
        previous = current
        current = following
    slope_val = resolution * (guesses * current - previous) / (guesses * guesses - 1.0)
    weights_q = 2.0 / ((1.0 - guesses * guesses) * slope_val * slope_val)
    return (guesses[::-1].copy(), weights_q[::-1].copy())

def legendre_table(resolution):
    points, quadrature = gauss_nodes(resolution)
    sine_row = np.sqrt(1.0 - points * points)
    basis = np.zeros((resolution, resolution, resolution))
    diagonal = np.full(resolution, math.sqrt(1.0 / (4.0 * math.pi)))
    for harmonic in range(resolution):
        if harmonic > 0:
            diagonal = diagonal * sine_row * math.sqrt((2.0 * harmonic + 1.0) / (2.0 * harmonic))
        basis[harmonic, harmonic] = diagonal
        if harmonic + 1 < resolution:
            basis[harmonic, harmonic + 1] = points * math.sqrt(2.0 * harmonic + 3.0) * diagonal
        for degree in range(harmonic + 2, resolution):
            alpha_coef = math.sqrt((4.0 * degree * degree - 1.0) / (degree * degree - harmonic * harmonic))
            beta_coef = math.sqrt(((degree - 1.0) ** 2 - harmonic * harmonic) / (4.0 * (degree - 1.0) ** 2 - 1.0))
            basis[harmonic, degree] = alpha_coef * (points * basis[harmonic, degree - 1] - beta_coef * basis[harmonic, degree - 2])
    return basis * np.sqrt(2.0 * math.pi * quadrature)[None, None, :]

def longitude_table(longitudes, degrees):
    column = jnp.arange(2 * degrees, dtype=jnp.int32)
    harmonic = column // 2
    parity = column % 2
    sample = jnp.arange(longitudes, dtype=jnp.int32)
    phase_step = sample[:, None] * harmonic[None, :] % longitudes
    angles = phase_step.astype(jnp.float32) * (2.0 * math.pi / longitudes)
    scales = jnp.where(harmonic == 0, 1.0 / math.sqrt(longitudes), math.sqrt(2.0 / longitudes)).astype(jnp.float32)
    basis = jnp.where(parity[None, :] == 0, jnp.cos(angles), -jnp.sin(angles)) * scales[None, :]
    return basis.astype(jnp.bfloat16)

def normal_cdf(values):
    return 0.5 * (1.0 + lax.erf(values * (1.0 / math.sqrt(2.0))))

def gelu_value(values):
    return values * normal_cdf(values)

def gelu_slope(values):
    density = jnp.exp(-0.5 * values * values) * (1.0 / math.sqrt(2.0 * math.pi))
    return normal_cdf(values) + values * density

def as_float(values):
    return values.astype(jnp.float32)

def analyse(field_in, polar_basis, long_basis):
    spectral = jnp.einsum('sanc,nk->sakc', as_float(field_in), as_float(long_basis)).astype(jnp.bfloat16)
    samples, latitudes, columns, channels = spectral.shape
    shaped = spectral.reshape(samples, latitudes, columns // 2, 2 * channels)
    return jnp.einsum('mla,samx->mlsx', as_float(polar_basis), as_float(shaped)).astype(jnp.bfloat16)

def synthesise(coefficients, polar_basis, long_basis):
    grid_part = jnp.einsum('mla,mlsx->samx', as_float(polar_basis), as_float(coefficients)).astype(jnp.bfloat16)
    samples, latitudes, orders_all, packed = grid_part.shape
    grid_part = grid_part.reshape(samples, latitudes, 2 * orders_all, packed // 2)
    return jnp.einsum('sakc,nk->sanc', as_float(grid_part), as_float(long_basis))

def mix_channels(coefficients, weight, backward):
    orders_all, degrees, samples, packed = coefficients.shape
    reshaped = as_float(coefficients.reshape(orders_all, degrees, samples, 2, packed // 2))
    if backward:
        mixed_coef = jnp.einsum('mlspd,lcd->mlspc', reshaped, as_float(weight))
    else:
        mixed_coef = jnp.einsum('mlspc,lcd->mlspd', reshaped, as_float(weight))
    return mixed_coef.astype(jnp.bfloat16).reshape(orders_all, degrees, samples, packed)

def degree_products(coefficients, gradients):
    orders_all, degrees, samples, packed = coefficients.shape
    left_side = as_float(coefficients.reshape(orders_all, degrees, samples, 2, packed // 2))
    right_side = as_float(gradients.reshape(orders_all, degrees, samples, 2, packed // 2))
    return jnp.einsum('mlspc,mlspd->lcd', left_side, right_side)

def reference(fields_in, cotangent, weights):
    polar_basis = jnp.asarray(legendre_table(DEGREES), jnp.float32).astype(jnp.bfloat16)
    long_basis = longitude_table(LONGITUDES, DEGREES)
    hidden_state = fields_in
    stored = []
    for layer_index in range(2):
        coefficients = analyse(hidden_state, polar_basis, long_basis)
        mixed_coef = mix_channels(coefficients, weights[layer_index], False)
        preact = synthesise(mixed_coef, polar_basis, long_basis)
        stored.append((coefficients, preact))
        hidden_state = (as_float(hidden_state) + gelu_value(preact)).astype(jnp.bfloat16)
    final_out = hidden_state
    upstream = cotangent
    grad_list = [None, None]
    for layer_index in (1, 0):
        coefficients, preact = stored[layer_index]
        grad_pre = (as_float(upstream) * gelu_slope(preact)).astype(jnp.bfloat16)
        grad_mixed = analyse(grad_pre, polar_basis, long_basis)
        grad_coef = mix_channels(grad_mixed, weights[layer_index], True)
        returned = synthesise(grad_coef, polar_basis, long_basis)
        grad_list[layer_index] = degree_products(coefficients, grad_mixed) / BATCH
        upstream = (as_float(upstream) + returned).astype(jnp.bfloat16)
    section_ends = jnp.stack([upstream, final_out])
    weight_grads = jnp.stack(grad_list)
    return (section_ends, weight_grads)
```

```python
import math

import jax
import jax.numpy as jnp
import ml_dtypes
import numpy as np
from jax import lax
from jax.experimental import pallas as pl
from jax.experimental.pallas import tpu as pltpu
from jax.sharding import PartitionSpec as P

BF16 = jnp.bfloat16
F32 = jnp.float32


def gauss_nodes(resolution):
    counter = np.arange(resolution) * 1.0
    guesses = np.cos(math.pi * (counter + 0.75) / (resolution + 0.5))
    for sweep in range(100):
        current = np.ones(resolution)
        previous = np.zeros(resolution)
        for degree in range(1, resolution + 1):
            following = (
                (2.0 * degree - 1.0) * guesses * current - (degree - 1.0) * previous
            ) / degree
            previous = current
            current = following
        slope_val = resolution * (guesses * current - previous) / (guesses * guesses - 1.0)
        guesses = guesses - current / slope_val
    current = np.ones(resolution)
    previous = np.zeros(resolution)
    for degree in range(1, resolution + 1):
        following = ((2.0 * degree - 1.0) * guesses * current - (degree - 1.0) * previous) / degree
        previous = current
        current = following
    slope_val = resolution * (guesses * current - previous) / (guesses * guesses - 1.0)
    weights_q = 2.0 / ((1.0 - guesses * guesses) * slope_val * slope_val)
    return (guesses[::-1].copy(), weights_q[::-1].copy())


def legendre_table(resolution):
    points, quadrature = gauss_nodes(resolution)
    sine_row = np.sqrt(1.0 - points * points)
    basis = np.zeros((resolution, resolution, resolution))
    diagonal = np.full(resolution, math.sqrt(1.0 / (4.0 * math.pi)))
    for harmonic in range(resolution):
        if harmonic > 0:
            diagonal = diagonal * sine_row * math.sqrt((2.0 * harmonic + 1.0) / (2.0 * harmonic))
        basis[harmonic, harmonic] = diagonal
        if harmonic + 1 < resolution:
            basis[harmonic, harmonic + 1] = points * math.sqrt(2.0 * harmonic + 3.0) * diagonal
        for degree in range(harmonic + 2, resolution):
            alpha_coef = math.sqrt(
                (4.0 * degree * degree - 1.0) / (degree * degree - harmonic * harmonic)
            )
            beta_coef = math.sqrt(
                ((degree - 1.0) ** 2 - harmonic * harmonic) / (4.0 * (degree - 1.0) ** 2 - 1.0)
            )
            basis[harmonic, degree] = alpha_coef * (
                points * basis[harmonic, degree - 1] - beta_coef * basis[harmonic, degree - 2]
            )
    return basis * np.sqrt(2.0 * math.pi * quadrature)[None, None, :]


def longitude_table(longitudes, degrees):
    column = np.arange(2 * degrees)
    harmonic, parity = column // 2, column % 2
    phase = (np.arange(longitudes)[:, None] * harmonic[None, :]) % longitudes
    angles = phase.astype(np.float32) * np.float32(2.0 * math.pi / longitudes)
    scales = np.where(harmonic == 0, 1.0 / math.sqrt(longitudes), math.sqrt(2.0 / longitudes))
    basis = np.where(parity[None, :] == 0, np.cos(angles), -np.sin(angles))
    return (basis * scales[None, :].astype(np.float32)).astype(ml_dtypes.bfloat16)


def polar_tables(degrees, shards):
    leg = legendre_table(degrees).astype(np.float32).astype(ml_dtypes.bfloat16)
    orders = degrees // shards
    wide = 2 * orders
    table = np.zeros((shards, degrees, wide, degrees, wide), ml_dtypes.bfloat16)
    for shard in range(shards):
        for k in range(wide):
            table[shard, :, k, :, k] = leg[shard * orders + k // 2]
    return table.reshape(shards, degrees * wide, degrees * wide)


def params(megabytes=48):
    return pltpu.CompilerParams(vmem_limit_bytes=megabytes * 2**20)


def dot(left, right):
    return jnp.dot(left, right, preferred_element_type=F32)


def normal_cdf(values):
    return 0.5 * (1.0 + lax.erf(values * (1.0 / math.sqrt(2.0))))


def store_analysis(spectra, out_ref):
    shards = out_ref.shape[0]
    wide = spectra[0].shape[0] // shards
    for d in range(shards):
        rows = [s[d * wide : (d + 1) * wide] for s in spectra]
        out_ref[d, 0] = jnp.concatenate(rows, axis=0).astype(BF16)


def load_spectra(in_ref):
    shards, _, rows, _ = in_ref.shape
    wide = 128 // shards
    blocks = [in_ref[d, 0].astype(F32) for d in range(shards)]
    return [
        jnp.concatenate([b[a * wide : (a + 1) * wide] for b in blocks], axis=0).astype(BF16)
        for a in range(rows // wide)
    ]


def first_body(idx_ref, field_ref, ana_ref, out_ref):
    basis = ana_ref[...]
    store_analysis([dot(basis, field_ref[0, a]) for a in range(field_ref.shape[1])], out_ref)


def layer0_body(idx_ref, in_ref, field_ref, syn_ref, ana_ref, h_ref, slope_ref, out_ref):
    syn, ana = syn_ref[...], ana_ref[...]
    spectra = []
    for a, spec in enumerate(load_spectra(in_ref)):
        pre = dot(syn, spec)
        cdf = normal_cdf(pre)
        density = jnp.exp(-0.5 * pre * pre) * (1.0 / math.sqrt(2.0 * math.pi))
        slope_ref[0, a] = (cdf + pre * density).astype(BF16)
        h = (field_ref[0, a].astype(F32) + pre * cdf).astype(BF16)
        h_ref[0, a] = h
        spectra.append(dot(ana, h))
    store_analysis(spectra, out_ref)


def layer1_body(idx_ref, in_ref, h_ref, cot_ref, syn_ref, ana_ref, top_ref, out_ref):
    syn, ana = syn_ref[...], ana_ref[...]
    spectra = []
    for a, spec in enumerate(load_spectra(in_ref)):
        pre = dot(syn, spec)
        cdf = normal_cdf(pre)
        density = jnp.exp(-0.5 * pre * pre) * (1.0 / math.sqrt(2.0 * math.pi))
        top_ref[0, a] = (h_ref[0, a].astype(F32) + pre * cdf).astype(BF16)
        gpre = (cot_ref[0, a].astype(F32) * (cdf + pre * density)).astype(BF16)
        spectra.append(dot(ana, gpre))
    store_analysis(spectra, out_ref)


def back1_body(idx_ref, in_ref, cot_ref, slope_ref, syn_ref, ana_ref, g_ref, out_ref):
    syn, ana = syn_ref[...], ana_ref[...]
    spectra = []
    for a, spec in enumerate(load_spectra(in_ref)):
        g = (cot_ref[0, a].astype(F32) + dot(syn, spec)).astype(BF16)
        g_ref[0, a] = g
        gpre = (g.astype(F32) * slope_ref[0, a].astype(F32)).astype(BF16)
        spectra.append(dot(ana, gpre))
    store_analysis(spectra, out_ref)


def back0_body(idx_ref, in_ref, g_ref, syn_ref, out_ref):
    syn = syn_ref[...]
    for a, spec in enumerate(load_spectra(in_ref)):
        out_ref[0, a] = (g_ref[0, a].astype(F32) + dot(syn, spec)).astype(BF16)


def mix_body(layer, backward, chunks, idx_ref, in_ref, fwd_ref, bwd_ref, own_ref, far_ref, *rest):
    rest = rest if len(rest) == 5 else rest[1:]
    coef_ref, out_ref, w_ref, mixed_ref, sem = rest
    shards, samples, rows, channels = in_ref.shape
    degrees = w_ref.shape[0]
    wide = fwd_ref.shape[1] // degrees
    step = degrees // chunks

    def fetch(c, source):
        span = pl.ds(c * step, step)
        return pltpu.make_async_copy(source.at[0, span], w_ref.at[span], sem.at[c])

    mine = idx_ref[1] == layer

    @pl.when(mine)
    def _():
        for c in range(chunks):
            fetch(c, own_ref).start()

    @pl.when(jnp.logical_not(mine))
    def _():
        for c in range(chunks):
            fetch(c, far_ref).start()

    forward = fwd_ref[0]
    for pair in range(0, samples, 2):
        both = []
        for s in (pair, pair + 1):
            flat = in_ref[:, s].reshape(shards * rows, channels)
            both.append(dot(forward, flat).reshape(degrees, wide, channels))
        coef_ref[:, pair * wide : (pair + 2) * wide] = jnp.concatenate(both, axis=1).astype(BF16)
    contract = (((1,), (1 if backward else 0,)), ((), ()))
    for c in range(chunks):
        fetch(c, own_ref).wait()
        for l in range(c * step, (c + 1) * step):
            mixed = lax.dot_general(coef_ref[l], w_ref[l], contract, preferred_element_type=F32)
            for s in range(samples):
                mixed_ref[s, l * wide : (l + 1) * wide] = mixed[s * wide : (s + 1) * wide]
    inverse = bwd_ref[0]
    for s in range(samples):
        grid = dot(inverse, mixed_ref[s].astype(BF16)).astype(BF16)
        out_ref[:, s] = grid.reshape(shards, rows, channels)


def local(polar, polar_t, fields_in, cotangent, weights):
    rows_all, lat_rows, longitudes, channels = fields_in.shape
    degrees = longitudes // 2
    shards = lax.axis_size("sht")
    samples = rows_all // 2
    wide = 2 * degrees // shards
    rows = lat_rows * wide
    section = lax.axis_index("section")
    idx = jnp.stack([lax.axis_index("sht"), section]).astype(jnp.int32)
    syn_np = longitude_table(longitudes, degrees)
    syn = jnp.asarray(syn_np)
    ana = jnp.asarray(np.ascontiguousarray(syn_np.T))

    grid_block = (1, lat_rows, longitudes, channels)
    spec_block = (shards, 1, rows, channels)
    half = pl.BlockSpec(grid_block, lambda s, i: (s + i[1] * samples, 0, 0, 0))
    field = pl.BlockSpec(grid_block, lambda s, i: (s, 0, 0, 0))
    spectral = pl.BlockSpec(spec_block, lambda s, i: (0, s, 0, 0))
    basis = pl.BlockSpec((longitudes, longitudes), lambda s, i: (0, 0))
    field_shape = jax.ShapeDtypeStruct((samples, lat_rows, longitudes, channels), BF16)
    spec_shape = jax.ShapeDtypeStruct((shards, samples, rows, channels), BF16)

    def grid_call(body, ins, outs, shapes, *args):
        return pl.pallas_call(
            body,
            grid_spec=pltpu.PrefetchScalarGridSpec(
                num_scalar_prefetch=1, grid=(samples,), in_specs=ins, out_specs=outs
            ),
            out_shape=shapes,
            compiler_params=params(),
        )(idx, *args)

    full = pl.BlockSpec((shards, samples, rows, channels), lambda t, i: (0, 0, 0, 0))
    size = degrees * wide
    table = pl.BlockSpec((1, size, size), lambda t, i: (i[0], 0, 0))
    anywhere = pl.BlockSpec(memory_space=pl.ANY)
    height = samples * wide
    chunks = 8

    def mix_call(slot, layer, backward, value, own, far, held):
        ins = [full, table, table, anywhere, anywhere]
        args = [value, polar, polar_t, own, far]
        alias = {}
        if held is not None:
            ins.append(anywhere)
            args.append(held)
            alias = {6: 0}

        def body(*refs):
            mix_body(layer, backward, chunks, *refs)

        return pl.pallas_call(
            body,
            grid_spec=pltpu.PrefetchScalarGridSpec(
                num_scalar_prefetch=1,
                grid=(1,),
                in_specs=ins,
                out_specs=[
                    pl.BlockSpec((degrees, height, channels), lambda t, i: (0, slot, 0)),
                    full,
                ],
                scratch_shapes=[
                    pltpu.VMEM((degrees, channels, channels), BF16),
                    pltpu.VMEM((samples, size, channels), F32),
                    pltpu.SemaphoreType.DMA((chunks,)),
                ],
            ),
            out_shape=[
                jax.ShapeDtypeStruct((degrees, 4 * height, channels), BF16),
                spec_shape,
            ],
            input_output_aliases=alias,
            compiler_params=params(),
        )(idx, *args)

    def turn(value):
        return lax.all_to_all(value, "sht", 0, 0, tiled=True)

    far = lax.ppermute(weights, "section", [(0, 1), (1, 0)])
    value = grid_call(first_body, [half, basis], spectral, spec_shape, fields_in, ana)
    held, value = mix_call(0, 0, False, turn(value), weights, far, None)
    h1, slope, value = grid_call(
        layer0_body,
        [spectral, half, basis, basis],
        [field, field, spectral],
        [field_shape, field_shape, spec_shape],
        turn(value), fields_in, syn, ana,
    )
    held, value = mix_call(1, 1, False, turn(value), weights, far, held)
    top, value = grid_call(
        layer1_body,
        [spectral, field, half, basis, basis],
        [field, spectral],
        [field_shape, spec_shape],
        turn(value), h1, cotangent, syn, ana,
    )
    held, value = mix_call(3, 1, True, turn(value), weights, far, held)
    g1, value = grid_call(
        back1_body,
        [spectral, half, field, basis, basis],
        [field, spectral],
        [field_shape, spec_shape],
        turn(value), cotangent, slope, syn, ana,
    )
    held, value = mix_call(2, 0, True, turn(value), weights, far, held)
    value, held = lax.optimization_barrier((turn(value), held))
    bottom = grid_call(
        back0_body, [spectral, field, basis], field, field_shape, value, g1, syn
    )
    front = section == 0
    passed = lax.ppermute(jnp.where(front, top, bottom), "section", [(0, 1), (1, 0)])
    section_ends = jnp.concatenate(
        [jnp.where(front, bottom, passed), jnp.where(front, passed, top)], axis=0
    )[None]

    owned = lax.all_to_all(held, ("sht", "dp"), 0, 0, tiled=True)
    owned = owned.reshape(-1, 4, height, channels)

    def product(j):
        return jnp.einsum(
            "irc,ird->cd", owned[:, j], owned[:, j + 2], preferred_element_type=F32
        )

    first, second = product(0), product(1)
    keep = jnp.where(front, first, second)
    give = jnp.where(front, second, first)
    total = keep + lax.ppermute(give, "section", [(0, 1), (1, 0)])
    batch_count = rows_all * lax.axis_size("dp")
    return (section_ends, (total / batch_count)[None, None])


def solution(mesh):
    in_specs = (
        P("dp", "sht", None, None),
        P("dp", "sht", None, None),
        P("section", None, None, None),
    )
    out_specs = (P("section", "dp", "sht", None, None), P("section", ("sht", "dp"), None, None))
    shards = mesh.shape["sht"]
    table = polar_tables(64, shards)
    table_t = np.ascontiguousarray(table.transpose(0, 2, 1))

    def body(fields_in, cotangent, weights):
        return local(jnp.asarray(table), jnp.asarray(table_t), fields_in, cotangent, weights)

    return jax.shard_map(body, mesh=mesh, in_specs=in_specs, out_specs=out_specs, check_vma=False)
```

```python
import math

import jax
import jax.numpy as jnp
import ml_dtypes
import numpy as np
from jax import lax
from jax.experimental import pallas as pl
from jax.experimental.pallas import tpu as pltpu
from jax.sharding import Mesh
from jax.sharding import PartitionSpec as P

BF16 = jnp.bfloat16
F32 = jnp.float32


def gauss_nodes(resolution):
    counter = np.arange(resolution) * 1.0
    guesses = np.cos(math.pi * (counter + 0.75) / (resolution + 0.5))
    for sweep in range(100):
        current = np.ones(resolution)
        previous = np.zeros(resolution)
        for degree in range(1, resolution + 1):
            following = (
                (2.0 * degree - 1.0) * guesses * current - (degree - 1.0) * previous
            ) / degree
            previous = current
            current = following
        slope_val = resolution * (guesses * current - previous) / (guesses * guesses - 1.0)
        guesses = guesses - current / slope_val
    current = np.ones(resolution)
    previous = np.zeros(resolution)
    for degree in range(1, resolution + 1):
        following = ((2.0 * degree - 1.0) * guesses * current - (degree - 1.0) * previous) / degree
        previous = current
        current = following
    slope_val = resolution * (guesses * current - previous) / (guesses * guesses - 1.0)
    weights_q = 2.0 / ((1.0 - guesses * guesses) * slope_val * slope_val)
    return (guesses[::-1].copy(), weights_q[::-1].copy())


def legendre_table(resolution):
    points, quadrature = gauss_nodes(resolution)
    sine_row = np.sqrt(1.0 - points * points)
    basis = np.zeros((resolution, resolution, resolution))
    diagonal = np.full(resolution, math.sqrt(1.0 / (4.0 * math.pi)))
    for harmonic in range(resolution):
        if harmonic > 0:
            diagonal = diagonal * sine_row * math.sqrt((2.0 * harmonic + 1.0) / (2.0 * harmonic))
        basis[harmonic, harmonic] = diagonal
        if harmonic + 1 < resolution:
            basis[harmonic, harmonic + 1] = points * math.sqrt(2.0 * harmonic + 3.0) * diagonal
        for degree in range(harmonic + 2, resolution):
            alpha_coef = math.sqrt(
                (4.0 * degree * degree - 1.0) / (degree * degree - harmonic * harmonic)
            )
            beta_coef = math.sqrt(
                ((degree - 1.0) ** 2 - harmonic * harmonic) / (4.0 * (degree - 1.0) ** 2 - 1.0)
            )
            basis[harmonic, degree] = alpha_coef * (
                points * basis[harmonic, degree - 1] - beta_coef * basis[harmonic, degree - 2]
            )
    return basis * np.sqrt(2.0 * math.pi * quadrature)[None, None, :]


def longitude_table(longitudes, degrees):
    column = np.arange(2 * degrees)
    harmonic, parity = column // 2, column % 2
    phase = (np.arange(longitudes)[:, None] * harmonic[None, :]) % longitudes
    angles = phase.astype(np.float32) * np.float32(2.0 * math.pi / longitudes)
    scales = np.where(harmonic == 0, 1.0 / math.sqrt(longitudes), math.sqrt(2.0 / longitudes))
    basis = np.where(parity[None, :] == 0, np.cos(angles), -np.sin(angles))
    return (basis * scales[None, :].astype(np.float32)).astype(ml_dtypes.bfloat16)


SLOTS = 72


def pair_degrees(degrees, blocks):
    quarter = degrees // 16
    return np.array(
        [
            16 * (r // quarter) + quarter * x + r % quarter
            for x in range(blocks)
            for r in range(degrees // 2 // blocks)
        ]
    )


def polar_tables(degrees, blocks):
    leg = legendre_table(degrees).astype(np.float32).astype(ml_dtypes.bfloat16)
    low = pair_degrees(degrees, blocks)
    pairs = degrees // 2
    ana = np.zeros((degrees + 1, 2, pairs, 2, pairs), ml_dtypes.bfloat16)
    syn = np.zeros((degrees, 2, pairs, 2, pairs), ml_dtypes.bfloat16)
    for half in range(2):
        for g, l in enumerate(low):
            for pos in range(degrees + 1):
                if l >= pos:
                    ana[pos, half, g, 0] = leg[pos, l, half::2]
                else:
                    ana[pos, half, g, 1] = leg[degrees - pos, degrees - 1 - l, half::2]
            for m in range(degrees):
                if l >= m:
                    syn[m, half, :, 0, g] = leg[m, l, half::2]
                if degrees - 1 - l >= m:
                    syn[m, half, :, 1, g] = leg[m, degrees - 1 - l, half::2]
    size = (2 * pairs, 2 * pairs)
    return ana.reshape((degrees + 1,) + size), syn.reshape((degrees,) + size)


def params(megabytes=48):
    return pltpu.CompilerParams(vmem_limit_bytes=megabytes * 2**20)


def dot(left, right):
    return jnp.dot(left, right, preferred_element_type=F32)


def normal_cdf(values):
    return 0.5 * (1.0 + lax.erf(values * (1.0 / math.sqrt(2.0))))


def low_lanes(shape):
    return lax.broadcasted_iota(jnp.int32, shape, len(shape) - 1) < shape[-1] // 2


def turned(value):
    return pltpu.roll(value, value.shape[-1] // 2, value.ndim - 1)


def interleave(first, second):
    low = low_lanes(first.shape)
    return jnp.where(low, first, turned(second)), jnp.where(low, turned(first), second)


def pack_body(idx_ref, field_ref, out_ref):
    _, rows, _, channels = field_ref.shape
    for q in range(rows // 2):
        one = field_ref[0, 2 * q].astype(F32)
        two = field_ref[0, 2 * q + 1].astype(F32)
        for t in range(channels // 128):
            span = slice(t * 128, (t + 1) * 128)
            left, right = interleave(one[:, span], two[:, span])
            out_ref[2 * t, q] = left.astype(BF16)
            out_ref[2 * t + 1, q] = right.astype(BF16)


def unpack_body(idx_ref, own_ref, far_ref, out_ref):
    _, rows, _, channels = out_ref.shape
    mine = (pl.program_id(0) // 4) == idx_ref[1]

    def write(ref):
        for q in range(rows // 2):
            for t in range(channels // 128):
                span = slice(t * 128, (t + 1) * 128)
                one, two = interleave(ref[2 * t, q].astype(F32), ref[2 * t + 1, q].astype(F32))
                out_ref[0, 2 * q, :, span] = one.astype(BF16)
                out_ref[0, 2 * q + 1, :, span] = two.astype(BF16)

    @pl.when(mine)
    def _():
        write(own_ref)

    @pl.when(jnp.logical_not(mine))
    def _():
        write(far_ref)


def repeat(count, body, unroll):
    def step(i, carry):
        body(i)
        return carry

    lax.fori_loop(0, count, step, 0, unroll=unroll)


def store_spectrum(q, value, spec_ref):
    spec_ref[pl.ds(q, 128, stride=32), :] = value


def analyse(spec_ref, table_ref, slot_ref, out_ref):
    degrees = table_ref.shape[0] - 1
    pairs = degrees // 2

    def slot(pos):
        m0 = jnp.minimum(pos, degrees - 1)
        m1 = jnp.minimum(degrees - pos, degrees - 1)
        one = spec_ref[pl.ds(pl.multiple_of(m0 * 64, 64), 64), :].astype(BF16)
        two = spec_ref[pl.ds(pl.multiple_of(m1 * 64, 64), 64), :].astype(BF16)
        right = jnp.concatenate(
            [
                jnp.concatenate([one[:pairs], two[:pairs]], axis=0),
                jnp.concatenate([one[pairs:], two[pairs:]], axis=0),
            ],
            axis=1,
        )
        both = dot(table_ref[pos], right)
        even, odd = both[:pairs], both[pairs:]
        low = low_lanes((pairs, 128))
        value = jnp.where(low, even[:, :128], odd[:, 128:]) + turned(
            jnp.where(low, even[:, 128:], odd[:, :128])
        )
        slot_ref[pl.ds(pos, pairs, stride=SLOTS), :] = value

    repeat(degrees + 1, slot, 5)
    for pos in range(degrees + 1, SLOTS):
        slot_ref[pl.ds(pos, pairs, stride=SLOTS), :] = jnp.zeros((pairs, 128), F32)
    blocks, rows, _ = out_ref.shape
    for b in range(blocks):
        out_ref[b] = slot_ref[b * rows : (b + 1) * rows, :].astype(BF16)


def synthesise(in_ref, table_ref, slot_ref, grid_ref):
    degrees = table_ref.shape[0]
    pairs = degrees // 2
    blocks, rows, _ = in_ref.shape
    for b in range(blocks):
        slot_ref[b * rows : (b + 1) * rows, :] = in_ref[b].astype(F32)

    def order(m):
        one = slot_ref[pl.ds(m, pairs, stride=SLOTS), :]
        two = slot_ref[pl.ds(degrees - m, pairs, stride=SLOTS), :]
        both = dot(table_ref[m], jnp.concatenate([one, two], axis=0).astype(BF16))
        real, imag = interleave(both[:pairs], both[pairs:])
        grid_ref[pl.ds(2 * m, pairs, stride=2 * degrees), :] = real
        grid_ref[pl.ds(2 * m + 1, pairs, stride=2 * degrees), :] = imag

    repeat(degrees, order, 4)


def spectrum_at(q, grid_ref):
    return grid_ref[pl.ds(pl.multiple_of(q * 128, 128), 128), :].astype(BF16)


def first_body(field_ref, ana_ref, ta_ref, out_ref, spec_ref, slot_ref):
    basis = ana_ref[...]
    repeat(field_ref.shape[0], lambda q: store_spectrum(q, dot(basis, field_ref[q]), spec_ref), 4)
    analyse(spec_ref, ta_ref, slot_ref, out_ref)


def layer0_body(in_ref, field_ref, syn_ref, ana_ref, ts_ref, ta_ref, h_ref, slope_ref, out_ref,
                spec_ref, grid_ref, slot_ref):
    synthesise(in_ref, ts_ref, slot_ref, grid_ref)
    syn, ana = syn_ref[...], ana_ref[...]

    def row(q):
        pre = dot(syn, spectrum_at(q, grid_ref))
        cdf = normal_cdf(pre)
        density = jnp.exp(-0.5 * pre * pre) * (1.0 / math.sqrt(2.0 * math.pi))
        slope_ref[q] = (cdf + pre * density).astype(BF16)
        h = (field_ref[q].astype(F32) + pre * cdf).astype(BF16)
        h_ref[q] = h
        store_spectrum(q, dot(ana, h), spec_ref)

    repeat(field_ref.shape[0], row, 2)
    analyse(spec_ref, ta_ref, slot_ref, out_ref)


def layer1_body(in_ref, h_ref, cot_ref, syn_ref, ana_ref, ts_ref, ta_ref, top_ref, out_ref,
                spec_ref, grid_ref, slot_ref):
    synthesise(in_ref, ts_ref, slot_ref, grid_ref)
    syn, ana = syn_ref[...], ana_ref[...]

    def row(q):
        pre = dot(syn, spectrum_at(q, grid_ref))
        cdf = normal_cdf(pre)
        density = jnp.exp(-0.5 * pre * pre) * (1.0 / math.sqrt(2.0 * math.pi))
        top_ref[q] = (h_ref[q].astype(F32) + pre * cdf).astype(BF16)
        gpre = (cot_ref[q].astype(F32) * (cdf + pre * density)).astype(BF16)
        store_spectrum(q, dot(ana, gpre), spec_ref)

    repeat(h_ref.shape[0], row, 2)
    analyse(spec_ref, ta_ref, slot_ref, out_ref)


def back1_body(in_ref, cot_ref, slope_ref, syn_ref, ana_ref, ts_ref, ta_ref, g_ref, out_ref,
               spec_ref, grid_ref, slot_ref):
    synthesise(in_ref, ts_ref, slot_ref, grid_ref)
    syn, ana = syn_ref[...], ana_ref[...]

    def row(q):
        g = (cot_ref[q].astype(F32) + dot(syn, spectrum_at(q, grid_ref))).astype(BF16)
        g_ref[q] = g
        gpre = (g.astype(F32) * slope_ref[q].astype(F32)).astype(BF16)
        store_spectrum(q, dot(ana, gpre), spec_ref)

    repeat(cot_ref.shape[0], row, 2)
    analyse(spec_ref, ta_ref, slot_ref, out_ref)


def back0_body(in_ref, g_ref, syn_ref, ts_ref, out_ref, grid_ref, slot_ref):
    synthesise(in_ref, ts_ref, slot_ref, grid_ref)
    syn = syn_ref[...]

    def row(q):
        out_ref[q] = (g_ref[q].astype(F32) + dot(syn, spectrum_at(q, grid_ref))).astype(BF16)

    repeat(g_ref.shape[0], row, 2)


def mix_body(layer, backward, idx_ref, in_ref, own_ref, far_ref, *rest):
    if backward:
        coef_ref, out_ref, grad_ref, w_ref, sem = rest
    else:
        out_ref, coef_ref, w_ref, sem = rest
    pairs = w_ref.shape[1]
    mine = idx_ref[1] == layer

    def fetch(source):
        return pltpu.make_async_copy(source, w_ref, sem)

    @pl.when(mine)
    def _():
        fetch(own_ref).start()

    @pl.when(jnp.logical_not(mine))
    def _():
        fetch(far_ref).start()

    contract = (((1,), (1 if backward else 0,)), ((), ()))
    rows = 2 * SLOTS
    index = lax.broadcasted_iota(jnp.int32, (rows, 256), 0)
    pos = jnp.where(index < SLOTS, index, index - SLOTS)
    stacks = []
    for rr in range(pairs // 2):
        span = slice(rr * rows, (rr + 1) * rows)
        blocks = [in_ref[b, span].astype(F32) for b in range(4)]
        a0, a1 = interleave(blocks[0], blocks[1])
        b0, b1 = interleave(blocks[2], blocks[3])
        real = jnp.concatenate([a0, b0], axis=1)
        imag = jnp.concatenate([a1, b1], axis=1)
        for i in range(2):
            part = slice(i * SLOTS, (i + 1) * SLOTS)
            stack = jnp.concatenate([real[part], imag[part]], axis=0)
            stacks.append(stack)
            if not backward:
                coef_ref[2 * rr + i] = stack.astype(BF16)
    fetch(own_ref).wait()
    for rr in range(pairs // 2):
        span = slice(rr * rows, (rr + 1) * rows)
        real, imag = [], []
        for r in (2 * rr, 2 * rr + 1):
            stack = stacks[r]
            narrow = stack.astype(BF16)
            lower = pos <= 16 * (r // 4) + r % 4 + 4 * idx_ref[0]
            one = lax.dot_general(narrow, w_ref[0, r], contract, preferred_element_type=F32)
            two = lax.dot_general(
                narrow, w_ref[1, pairs - 1 - r], contract, preferred_element_type=F32
            )
            mixed = jnp.where(lower, one, two)
            real.append(mixed[:SLOTS])
            imag.append(mixed[SLOTS:])
            if backward:
                over = (((0,), (0,)), ((), ()))
                first = jnp.where(lower, stack, 0.0).astype(BF16)
                second = jnp.where(lower, 0.0, stack).astype(BF16)
                for place, piece in ((r, first), (2 * pairs - 1 - r, second)):
                    grad = lax.dot_general(coef_ref[r], piece, over, preferred_element_type=F32)
                    grad_ref[place] = grad.astype(BF16)
        real = jnp.concatenate(real, axis=0)
        imag = jnp.concatenate(imag, axis=0)
        for t in range(2):
            lanes = slice(t * 128, (t + 1) * 128)
            left, right = interleave(real[:, lanes], imag[:, lanes])
            out_ref[2 * t, span] = left.astype(BF16)
            out_ref[2 * t + 1, span] = right.astype(BF16)


def local(ta, ts, fields_in, cotangent, weights):
    rows_all, lat_rows, longitudes, channels = fields_in.shape
    degrees = longitudes // 2
    samples = rows_all // 2
    section = lax.axis_index("section")
    x_at, z_at = lax.axis_index("x"), lax.axis_index("z")
    idx = jnp.stack([x_at, section]).astype(jnp.int32)
    syn_np = longitude_table(longitudes, degrees)
    syn = jnp.asarray(syn_np)
    ana = jnp.asarray(np.ascontiguousarray(syn_np.T))
    swap = [(0, 1), (1, 0)]
    pairs = degrees // 2
    q_rows = lat_rows // 2
    block_rows = pairs // 4 * SLOTS

    packed_block = pl.BlockSpec((4, q_rows, longitudes, 128), lambda s, i: (s, 0, 0, 0))
    packed_shape = jax.ShapeDtypeStruct((16, q_rows, longitudes, 128), BF16)
    grid_shape = jax.ShapeDtypeStruct((pairs, longitudes, 128), BF16)
    spec_shape = jax.ShapeDtypeStruct((4, block_rows, 128), BF16)

    def pack(field):
        block = (1, lat_rows, longitudes, channels)
        return pl.pallas_call(
            pack_body,
            grid_spec=pltpu.PrefetchScalarGridSpec(
                num_scalar_prefetch=1,
                grid=(samples,),
                in_specs=[pl.BlockSpec(block, lambda s, i: (s + i[1] * samples, 0, 0, 0))],
                out_specs=packed_block,
            ),
            out_shape=packed_shape,
            compiler_params=params(),
        )(idx, field)

    def unpack(own, far):
        block = (1, lat_rows, longitudes, channels)
        held = pl.BlockSpec(
            (4, q_rows, longitudes, 128), lambda s, i: (lax.rem(s, samples), 0, 0, 0)
        )
        return pl.pallas_call(
            unpack_body,
            grid_spec=pltpu.PrefetchScalarGridSpec(
                num_scalar_prefetch=1,
                grid=(rows_all,),
                in_specs=[held, held],
                out_specs=pl.BlockSpec(block, lambda s, i: (s, 0, 0, 0)),
            ),
            out_shape=jax.ShapeDtypeStruct(fields_in.shape, BF16),
            compiler_params=params(),
        )(idx, own, far)

    def to_local(field):
        return lax.all_to_all(pack(field), ("z", "x"), 0, 0, tiled=True).reshape(grid_shape.shape)

    def to_rows(value):
        return lax.all_to_all(value.reshape(packed_shape.shape), ("z", "x"), 0, 0, tiled=True)

    def turn(value):
        return lax.all_to_all(value, "x", 0, 0, tiled=True)

    tall = pltpu.VMEM((pairs * 128, 128), F32)
    slots = pltpu.VMEM((pairs * SLOTS, 128), F32)

    def grid_call(body, shapes, scratch, *args):
        return pl.pallas_call(
            body, out_shape=shapes, scratch_shapes=scratch, compiler_params=params()
        )(*args)

    vmem = pl.BlockSpec(memory_space=pltpu.VMEM)
    anywhere = pl.BlockSpec(memory_space=pl.ANY)
    coef_shape = jax.ShapeDtypeStruct((pairs // 4, 2 * SLOTS, channels), BF16)
    grad_shape = jax.ShapeDtypeStruct((degrees // 4, channels, channels), BF16)

    def mix_call(layer, value, own, far, coef=None):
        backward = coef is not None

        def body(*refs):
            mix_body(layer, backward, *refs)

        return pl.pallas_call(
            body,
            in_specs=[pl.BlockSpec(memory_space=pltpu.SMEM), vmem, anywhere, anywhere]
            + [vmem] * backward,
            out_specs=[vmem, vmem],
            out_shape=[spec_shape, grad_shape if backward else coef_shape],
            scratch_shapes=[
                pltpu.VMEM((2, pairs // 4, channels, channels), BF16),
                pltpu.SemaphoreType.DMA,
            ],
            compiler_params=params(),
        )(idx, value, own, far, *([coef] if backward else []))

    folded = weights[0].reshape(4, 4, 4, channels, channels)
    low = lax.dynamic_index_in_dim(folded[:2], x_at, 1, keepdims=False)
    high = lax.dynamic_index_in_dim(folded[2:], 3 - x_at, 1, keepdims=False)
    own = jnp.stack([low, high]).reshape(2, pairs // 4, channels, channels)
    far = lax.ppermute(own, "section", swap)

    front = section == 0

    def reduce_first(grad):
        halves = grad.reshape(degrees // 4, 2, channels // 2, channels)
        keep = lax.dynamic_index_in_dim(halves, section, 1, keepdims=False)
        give = lax.dynamic_index_in_dim(halves, 1 - section, 1, keepdims=False)
        got = lax.ppermute(give, "section", swap)
        both = (keep.astype(F32) + got.astype(F32)).astype(BF16)
        parts = lax.all_to_all(both, ("z", "dp"), 0, 0, tiled=True)
        return jnp.sum(parts.astype(F32), axis=0)

    field = to_local(fields_in)
    value = grid_call(first_body, spec_shape, [tall, slots], field, ana, ta)
    cot = to_local(cotangent)
    value, coef0 = mix_call(0, turn(value), own, far)
    h1, slope, value = grid_call(
        layer0_body, [grid_shape, grid_shape, spec_shape], [tall, tall, slots],
        turn(value), field, syn, ana, ts, ta,
    )
    value, coef1 = mix_call(1, turn(value), own, far)
    top, value = grid_call(
        layer1_body, [grid_shape, spec_shape], [tall, tall, slots],
        turn(value), h1, cot, syn, ana, ts, ta,
    )
    value, grad1 = mix_call(1, turn(value), own, far, coef1)
    g1, value = grid_call(
        back1_body, [grid_shape, spec_shape], [tall, tall, slots],
        turn(value), cot, slope, syn, ana, ts, ta,
    )
    value, grad0 = mix_call(0, turn(value), own, far, coef0)
    bottom = grid_call(
        back0_body, grid_shape, [tall, slots], turn(value), g1, syn, ts
    )
    top = to_rows(top)
    bottom = to_rows(bottom)
    passed = lax.ppermute(jnp.where(front, top, bottom), "section", swap)
    section_ends = unpack(jnp.where(front, bottom, top), passed)[None]

    sum1, sum0 = reduce_first(grad1), reduce_first(grad0)
    mine = jnp.where(front, sum0, sum1)
    other = lax.ppermute(jnp.where(front, sum1, sum0), "section", swap)
    total = jnp.concatenate([jnp.where(front, mine, other), jnp.where(front, other, mine)], axis=0)
    flipped = lax.ppermute(total, "x", [(i, 3 - i) for i in range(4)])
    total = jnp.where(z_at < 2, total, flipped)
    batch_count = rows_all * lax.axis_size("dp")
    return (section_ends, (total / batch_count)[None, None])


def solution(mesh):
    grid = Mesh(mesh.devices.reshape(2, 4, 4, 4), ("section", "z", "x", "dp"))
    rows = P("dp", ("z", "x"), None, None)
    in_specs = (rows, rows, P("section", None, None, None))
    out_specs = (
        P("section", "dp", ("z", "x"), None, None),
        P("section", ("z", "x", "dp"), None, None),
    )
    ta, ts = polar_tables(64, 4)

    def body(fields_in, cotangent, weights):
        return local(jnp.asarray(ta), jnp.asarray(ts), fields_in, cotangent, weights)

    return jax.shard_map(body, mesh=grid, in_specs=in_specs, out_specs=out_specs, check_vma=False)
```

```python
import math

import jax
import jax.numpy as jnp
import ml_dtypes
import numpy as np
from jax import lax
from jax.experimental import pallas as pl
from jax.experimental.pallas import tpu as pltpu
from jax.sharding import Mesh
from jax.sharding import PartitionSpec as P

BF16 = jnp.bfloat16
F32 = jnp.float32


def gauss_nodes(resolution):
    counter = np.arange(resolution) * 1.0
    guesses = np.cos(math.pi * (counter + 0.75) / (resolution + 0.5))
    for sweep in range(100):
        current = np.ones(resolution)
        previous = np.zeros(resolution)
        for degree in range(1, resolution + 1):
            following = (
                (2.0 * degree - 1.0) * guesses * current - (degree - 1.0) * previous
            ) / degree
            previous = current
            current = following
        slope_val = resolution * (guesses * current - previous) / (guesses * guesses - 1.0)
        guesses = guesses - current / slope_val
    current = np.ones(resolution)
    previous = np.zeros(resolution)
    for degree in range(1, resolution + 1):
        following = ((2.0 * degree - 1.0) * guesses * current - (degree - 1.0) * previous) / degree
        previous = current
        current = following
    slope_val = resolution * (guesses * current - previous) / (guesses * guesses - 1.0)
    weights_q = 2.0 / ((1.0 - guesses * guesses) * slope_val * slope_val)
    return (guesses[::-1].copy(), weights_q[::-1].copy())


def legendre_table(resolution):
    points, quadrature = gauss_nodes(resolution)
    sine_row = np.sqrt(1.0 - points * points)
    basis = np.zeros((resolution, resolution, resolution))
    diagonal = np.full(resolution, math.sqrt(1.0 / (4.0 * math.pi)))
    for harmonic in range(resolution):
        if harmonic > 0:
            diagonal = diagonal * sine_row * math.sqrt((2.0 * harmonic + 1.0) / (2.0 * harmonic))
        basis[harmonic, harmonic] = diagonal
        if harmonic + 1 < resolution:
            basis[harmonic, harmonic + 1] = points * math.sqrt(2.0 * harmonic + 3.0) * diagonal
        for degree in range(harmonic + 2, resolution):
            alpha_coef = math.sqrt(
                (4.0 * degree * degree - 1.0) / (degree * degree - harmonic * harmonic)
            )
            beta_coef = math.sqrt(
                ((degree - 1.0) ** 2 - harmonic * harmonic) / (4.0 * (degree - 1.0) ** 2 - 1.0)
            )
            basis[harmonic, degree] = alpha_coef * (
                points * basis[harmonic, degree - 1] - beta_coef * basis[harmonic, degree - 2]
            )
    return basis * np.sqrt(2.0 * math.pi * quadrature)[None, None, :]


def longitude_table(longitudes, degrees):
    column = np.arange(2 * degrees)
    harmonic, parity = column // 2, column % 2
    phase = (np.arange(longitudes)[:, None] * harmonic[None, :]) % longitudes
    angles = phase.astype(np.float32) * np.float32(2.0 * math.pi / longitudes)
    scales = np.where(harmonic == 0, 1.0 / math.sqrt(longitudes), math.sqrt(2.0 / longitudes))
    basis = np.where(parity[None, :] == 0, np.cos(angles), -np.sin(angles))
    return (basis * scales[None, :].astype(np.float32)).astype(ml_dtypes.bfloat16)


SLOTS = 72


def pair_degrees(degrees, blocks):
    quarter = degrees // 16
    return np.array(
        [
            16 * (r // quarter) + quarter * x + r % quarter
            for x in range(blocks)
            for r in range(degrees // 2 // blocks)
        ]
    )


def polar_tables(degrees, blocks):
    leg = legendre_table(degrees).astype(np.float32).astype(ml_dtypes.bfloat16)
    low = pair_degrees(degrees, blocks)
    pairs = degrees // 2
    ana = np.zeros((degrees + 1, 2, pairs, 2, pairs), ml_dtypes.bfloat16)
    syn = np.zeros((degrees, 2, pairs, 2, pairs), ml_dtypes.bfloat16)
    for half in range(2):
        for g, l in enumerate(low):
            for pos in range(degrees + 1):
                if l >= pos:
                    ana[pos, half, g, 1] = leg[pos, l, half::2]
                else:
                    ana[pos, half, g, 0] = leg[degrees - pos, degrees - 1 - l, half::2]
            for m in range(degrees):
                if l >= m:
                    syn[m, half, :, 1, g] = leg[m, l, half::2]
                if degrees - 1 - l >= m:
                    syn[m, half, :, 0, g] = leg[m, degrees - 1 - l, half::2]
    size = (2 * pairs, 2 * pairs)
    return ana.reshape((degrees + 1,) + size), syn.reshape((degrees,) + size)


def params(megabytes=16):
    return pltpu.CompilerParams(vmem_limit_bytes=megabytes * 2**20)


def cost(microseconds):
    return pl.CostEstimate(
        flops=int(microseconds * 1.1e9), bytes_accessed=1 << 20, transcendentals=0
    )


def dot(left, right):
    return jnp.dot(left, right, preferred_element_type=F32)


def normal_cdf(values):
    return 0.5 * (1.0 + lax.erf(values * (1.0 / math.sqrt(2.0))))


def low_lanes(shape):
    return lax.broadcasted_iota(jnp.int32, shape, len(shape) - 1) < shape[-1] // 2


def turned(value):
    return pltpu.roll(value, value.shape[-1] // 2, value.ndim - 1)


def interleave(first, second):
    low = low_lanes(first.shape)
    return jnp.where(low, first, turned(second)), jnp.where(low, turned(first), second)


def begin(source, target, sem):
    copy = pltpu.make_async_copy(source, target, sem)
    copy.start()
    return copy


def pack_body(idx_ref, field_hbm, cot_hbm, out_ref, field_ref, cot_ref, sem):
    samples, rows, _, channels = field_ref.shape
    loads = []
    for s in range(samples):
        at = s + samples * idx_ref[1]
        loads.append(begin(field_hbm.at[at], field_ref.at[s], sem.at[s]))
        loads.append(begin(cot_hbm.at[at], cot_ref.at[s], sem.at[samples + s]))
    for s in range(samples):
        for i, ref in enumerate((field_ref, cot_ref)):
            loads[2 * s + i].wait()
            for q in range(rows // 2):
                for t in range(channels // 128):
                    span = slice(t * 128, (t + 1) * 128)
                    one, two = ref[s, 2 * q, :, span], ref[s, 2 * q + 1, :, span]
                    left, right = interleave(one.astype(F32), two.astype(F32))
                    out_ref[4 * s + 2 * t, i, q] = left.astype(BF16)
                    out_ref[4 * s + 2 * t + 1, i, q] = right.astype(BF16)


def unpack_body(in_ref, out_hbm, out_ref, sem):
    samples, rows, _, channels = out_ref.shape
    saves = []
    for s in range(samples):
        for q in range(rows // 2):
            for t in range(channels // 128):
                span = slice(t * 128, (t + 1) * 128)
                one, two = in_ref[4 * s + 2 * t, q], in_ref[4 * s + 2 * t + 1, q]
                one, two = interleave(one.astype(F32), two.astype(F32))
                out_ref[s, 2 * q, :, span] = one.astype(BF16)
                out_ref[s, 2 * q + 1, :, span] = two.astype(BF16)
        saves.append(begin(out_ref.at[s], out_hbm.at[s], sem.at[s]))
    for save in saves:
        save.wait()


def select_body(idx_ref, weight_ref, out_ref, sem):
    quarter = out_ref.shape[1] // 2
    copies = []
    for z in range(4):
        at = 4 * quarter * z + quarter * (idx_ref[0] if z < 2 else 3 - idx_ref[0])
        target = out_ref.at[z // 2, pl.ds((z % 2) * quarter, quarter)]
        copies.append(begin(weight_ref.at[0, pl.ds(at, quarter)], target, sem.at[z]))
    for copy in copies:
        copy.wait()


def prepare_body(idx_ref, own_ref, far_ref, ta_hbm, ts_hbm, w0_ref, w1_ref, ta_ref, ts_ref, sem):
    def fetch(source, target, at):
        return pltpu.make_async_copy(source, target, sem.at[at])

    tables = [begin(ta_hbm, ta_ref, sem.at[2]), begin(ts_hbm, ts_ref, sem.at[3])]

    @pl.when(idx_ref[1] == 0)
    def _():
        fetch(own_ref, w0_ref, 0).start()
        fetch(far_ref, w1_ref, 1).start()

    @pl.when(idx_ref[1] == 1)
    def _():
        fetch(far_ref, w0_ref, 0).start()
        fetch(own_ref, w1_ref, 1).start()

    fetch(own_ref, w0_ref, 0).wait()
    fetch(own_ref, w1_ref, 1).wait()
    for table in tables:
        table.wait()


def store_spectrum(q, value, spec_ref):
    spec_ref[pl.ds(q, 128, stride=32), :] = value


def spectrum_at(q, grid_ref):
    return grid_ref[q * 128 : (q + 1) * 128, :].astype(BF16)


def analyse(spec_ref, table_ref, slot_ref, out_ref):
    degrees = table_ref.shape[0] - 1
    pairs = degrees // 2

    low = low_lanes((pairs, 128))

    def order(m):
        rows = spec_ref[m * 2 * pairs : (m + 1) * 2 * pairs, :].astype(BF16)
        return jnp.concatenate([rows[:pairs], rows[pairs:]], axis=1)

    for pos in range(degrees + 1):
        right, left = order(min(degrees - pos, degrees - 1)), table_ref[pos]
        if pos < pairs:
            right = jnp.concatenate([right, order(pos)], axis=0)
        else:
            left = left[:, :pairs]
        both = dot(left, right)
        even, odd = both[:pairs], both[pairs:]
        value = jnp.where(low, even[:, :128], odd[:, 128:]) + turned(
            jnp.where(low, even[:, 128:], odd[:, :128])
        )
        slot_ref[pl.ds(pos, pairs, stride=SLOTS), :] = value
    for pos in range(degrees + 1, SLOTS):
        slot_ref[pl.ds(pos, pairs, stride=SLOTS), :] = jnp.zeros((pairs, 128), F32)
    blocks, rows, _ = out_ref.shape
    for b in range(blocks):
        out_ref[b] = slot_ref[b * rows : (b + 1) * rows, :].astype(BF16)


def synthesise(in_ref, table_ref, slot_ref, grid_ref):
    degrees = table_ref.shape[0]
    pairs = degrees // 2
    blocks, rows, _ = in_ref.shape
    for b in range(blocks):
        slot_ref[b * rows : (b + 1) * rows, :] = in_ref[b].astype(F32)

    for m in range(degrees):
        right = slot_ref[pl.ds(degrees - m, pairs, stride=SLOTS), :]
        left = table_ref[m]
        if m < pairs:
            low = slot_ref[pl.ds(m, pairs, stride=SLOTS), :]
            right = jnp.concatenate([right, low], axis=0)
        else:
            left = left[:, :pairs]
        both = dot(left, right.astype(BF16))
        real, imag = interleave(both[:pairs], both[pairs:])
        grid_ref[pl.ds(2 * m, pairs, stride=2 * degrees), :] = real
        grid_ref[pl.ds(2 * m + 1, pairs, stride=2 * degrees), :] = imag


def gelu_parts(pre):
    cdf = normal_cdf(pre)
    density = jnp.exp(-0.5 * pre * pre) * (1.0 / math.sqrt(2.0 * math.pi))
    return pre * cdf, cdf + pre * density


def first_body(recv_ref, ana_ref, ta_ref, out_ref, spec_ref, slot_ref):
    basis = ana_ref[...]
    for d in range(recv_ref.shape[0]):
        for q in range(2):
            store_spectrum(2 * d + q, dot(basis, recv_ref[d, 0, q]), spec_ref)
    analyse(spec_ref, ta_ref, slot_ref, out_ref)


def layer0_body(in_ref, recv_ref, syn_ref, ana_ref, ts_ref, ta_ref, h_ref, slope_ref, out_ref,
                spec_ref, grid_ref, slot_ref):
    synthesise(in_ref, ts_ref, slot_ref, grid_ref)
    syn, ana = syn_ref[...], ana_ref[...]
    for d in range(recv_ref.shape[0]):
        for q in range(2):
            value, slope = gelu_parts(dot(syn, spectrum_at(2 * d + q, grid_ref)))
            slope_ref[d, q] = slope.astype(BF16)
            h = (recv_ref[d, 0, q].astype(F32) + value).astype(BF16)
            h_ref[d, q] = h
            store_spectrum(2 * d + q, dot(ana, h), spec_ref)
    analyse(spec_ref, ta_ref, slot_ref, out_ref)


def layer1_body(in_ref, recv_ref, h_ref, syn_ref, ana_ref, ts_ref, ta_ref, top_ref, out_ref,
                spec_ref, grid_ref, slot_ref):
    synthesise(in_ref, ts_ref, slot_ref, grid_ref)
    syn, ana = syn_ref[...], ana_ref[...]
    for d in range(recv_ref.shape[0]):
        for q in range(2):
            value, slope = gelu_parts(dot(syn, spectrum_at(2 * d + q, grid_ref)))
            top_ref[d, q] = (h_ref[d, q].astype(F32) + value).astype(BF16)
            gpre = (recv_ref[d, 1, q].astype(F32) * slope).astype(BF16)
            store_spectrum(2 * d + q, dot(ana, gpre), spec_ref)
    analyse(spec_ref, ta_ref, slot_ref, out_ref)


def back1_body(in_ref, recv_ref, slope_ref, syn_ref, ana_ref, ts_ref, ta_ref, g_ref, out_ref,
               spec_ref, grid_ref, slot_ref):
    synthesise(in_ref, ts_ref, slot_ref, grid_ref)
    syn, ana = syn_ref[...], ana_ref[...]
    for d in range(recv_ref.shape[0]):
        for q in range(2):
            back = dot(syn, spectrum_at(2 * d + q, grid_ref))
            g = (recv_ref[d, 1, q].astype(F32) + back).astype(BF16)
            g_ref[d, q] = g
            gpre = (g.astype(F32) * slope_ref[d, q].astype(F32)).astype(BF16)
            store_spectrum(2 * d + q, dot(ana, gpre), spec_ref)
    analyse(spec_ref, ta_ref, slot_ref, out_ref)


def back0_body(in_ref, g_ref, top_ref, syn_ref, ts_ref, ends_ref, grid_ref, slot_ref, sem):
    move = begin(top_ref, ends_ref.at[1], sem.at[0])
    synthesise(in_ref, ts_ref, slot_ref, grid_ref)
    syn = syn_ref[...]
    for d in range(g_ref.shape[0]):
        for q in range(2):
            back = dot(syn, spectrum_at(2 * d + q, grid_ref))
            ends_ref[0, d, q] = (g_ref[d, q].astype(F32) + back).astype(BF16)
    move.wait()


def lower_rows(x_at, r):
    index = lax.broadcasted_iota(jnp.int32, (2 * SLOTS, 256), 0)
    pos = jnp.where(index < SLOTS, index, index - SLOTS)
    return pos <= 16 * (r // 4) + r % 4 + 4 * x_at


def mix_body(backward, idx_ref, in_ref, w_ref, out_ref, coef_ref):
    pairs = w_ref.shape[1]
    contract = (((1,), (1 if backward else 0,)), ((), ()))
    rows = 2 * SLOTS
    for rr in range(pairs // 2):
        span = slice(rr * rows, (rr + 1) * rows)
        blocks = [in_ref[b, span].astype(F32) for b in range(4)]
        a0, a1 = interleave(blocks[0], blocks[1])
        b0, b1 = interleave(blocks[2], blocks[3])
        real = jnp.concatenate([a0, b0], axis=1)
        imag = jnp.concatenate([a1, b1], axis=1)
        reals, imags = [], []
        for r in (2 * rr, 2 * rr + 1):
            part = slice((r % 2) * SLOTS, (r % 2 + 1) * SLOTS)
            stack = jnp.concatenate([real[part], imag[part]], axis=0).astype(BF16)
            coef_ref[r] = stack
            one = lax.dot_general(stack, w_ref[0, r], contract, preferred_element_type=F32)
            two = lax.dot_general(
                stack, w_ref[1, pairs - 1 - r], contract, preferred_element_type=F32
            )
            mixed = jnp.where(lower_rows(idx_ref[0], r), one, two)
            reals.append(mixed[:SLOTS])
            imags.append(mixed[SLOTS:])
        real = jnp.concatenate(reals, axis=0)
        imag = jnp.concatenate(imags, axis=0)
        for t in range(2):
            lanes = slice(t * 128, (t + 1) * 128)
            left, right = interleave(real[:, lanes], imag[:, lanes])
            out_ref[2 * t, span] = left.astype(BF16)
            out_ref[2 * t + 1, span] = right.astype(BF16)


def grad_body(flip, idx_ref, coef0_ref, coef1_ref, grad0_ref, grad1_ref, out_ref):
    pairs = coef0_ref.shape[0]
    over = (((0,), (0,)), ((), ()))
    first = idx_ref[1] == (1 if flip else 0)
    for r in range(pairs):
        coef = jnp.where(first, coef0_ref[r].astype(F32), coef1_ref[r].astype(F32)).astype(BF16)
        grad = jnp.where(first, grad0_ref[r].astype(F32), grad1_ref[r].astype(F32))
        lower = lower_rows(idx_ref[0], r)
        pieces = (jnp.where(lower, grad, 0.0), jnp.where(lower, 0.0, grad))
        for at, piece in zip((r, 2 * pairs - 1 - r), pieces):
            place = 4 * ((at % 4 + 4 - idx_ref[2]) % 4) + (at // 4 + 4 - idx_ref[3]) % 4
            made = lax.dot_general(coef, piece.astype(BF16), over, preferred_element_type=F32)
            out_ref[place] = made.astype(BF16)


def local(ta, ts, fields_in, cotangent, weights):
    rows_all, lat_rows, longitudes, channels = fields_in.shape
    degrees = longitudes // 2
    samples = rows_all // 2
    section = lax.axis_index("section")
    x_at, z_at, y_at = lax.axis_index("x"), lax.axis_index("z"), lax.axis_index("dp")
    idx = jnp.stack([x_at, section, y_at, z_at]).astype(jnp.int32)
    syn_np = longitude_table(longitudes, degrees)
    syn = jnp.asarray(syn_np)
    ana = jnp.asarray(np.ascontiguousarray(syn_np.T))
    swap = [(0, 1), (1, 0)]
    pairs = degrees // 2
    q_rows = lat_rows // 2

    vmem = pl.BlockSpec(memory_space=pltpu.VMEM)
    smem = pl.BlockSpec(memory_space=pltpu.SMEM)
    hbm = pl.BlockSpec(memory_space=pltpu.HBM)
    half_shape = (16, q_rows, longitudes, 128)
    half = pltpu.VMEM(half_shape, BF16)
    spec = pltpu.VMEM((4, pairs // 4 * SLOTS, 128), BF16)
    coef = pltpu.VMEM((pairs // 4, 2 * SLOTS, channels), BF16)
    product = pltpu.VMEM((degrees // 4, channels, channels), BF16)
    chosen = pltpu.VMEM((2, pairs // 4, channels, channels), BF16)
    tall = pltpu.VMEM((pairs * 128, 128), F32)
    slots = pltpu.VMEM((pairs * SLOTS, 128), F32)

    def far_away(array):
        return pltpu.with_memory_space_constraint(array, pltpu.HBM)

    def near(array):
        return pltpu.with_memory_space_constraint(array, pltpu.VMEM)

    def call(time, body, ins, shapes, scratches, *args, sems=0, outs=None):
        many = isinstance(shapes, list)
        return pl.pallas_call(
            body,
            in_specs=ins,
            out_specs=outs or ([vmem] * len(shapes) if many else vmem),
            out_shape=shapes,
            scratch_shapes=scratches + [pltpu.SemaphoreType.DMA((sems,))] * (sems > 0),
            cost_estimate=cost(time),
            compiler_params=params(),
        )(*args)

    quarter_field = pltpu.VMEM((samples, lat_rows, longitudes, channels), BF16)
    packed = call(
        3, pack_body, [smem, hbm, hbm], pltpu.VMEM((16, 2) + half_shape[1:], BF16),
        [quarter_field] * 2, idx, far_away(fields_in), far_away(cotangent), sems=2 * samples,
    )
    own = call(2, select_body, [smem, hbm], chosen, [], idx, far_away(weights), sems=4)
    far = lax.ppermute(own, "section", swap)
    w0, w1, ta, ts = call(
        2, prepare_body, [smem, vmem, vmem, hbm, hbm],
        [chosen, chosen, pltpu.VMEM(ta.shape, BF16), pltpu.VMEM(ts.shape, BF16)], [],
        idx, near(own), near(far), far_away(ta), far_away(ts), sems=4,
    )
    recv = near(lax.all_to_all(packed, ("z", "x"), 0, 0, tiled=True))

    def turn(value):
        return near(lax.all_to_all(value, "x", 0, 0, tiled=True))

    def mix_call(value, weight, backward):
        def body(*refs):
            mix_body(backward, *refs)

        return call(2, body, [smem, vmem, vmem], [spec, coef], [], idx, value, weight)

    value = call(3, first_body, [vmem] * 3, spec, [tall, slots], recv, ana, ta)
    value, coef0 = mix_call(turn(value), w0, False)
    h1, slope, value = call(
        6, layer0_body, [vmem] * 6, [half, half, spec], [tall, tall, slots],
        turn(value), recv, syn, ana, ts, ta,
    )
    value, coef1 = mix_call(turn(value), w1, False)
    top, value = call(
        6, layer1_body, [vmem] * 7, [half, spec], [tall, tall, slots],
        turn(value), recv, h1, syn, ana, ts, ta,
    )
    value, grad1 = mix_call(turn(value), w1, True)
    g1, value = call(
        5, back1_body, [vmem] * 7, [half, spec], [tall, tall, slots],
        turn(value), recv, slope, syn, ana, ts, ta,
    )
    value, grad0 = mix_call(turn(value), w0, True)
    ends = call(
        4, back0_body, [vmem] * 5, pltpu.VMEM((2,) + half_shape, BF16), [tall, slots],
        turn(value), g1, top, syn, ts, sems=1,
    )
    ends = ends.reshape((32,) + half_shape[1:])
    ends = near(lax.all_to_all(ends, ("section", "z", "x"), 0, 0, tiled=True))
    section_ends = call(
        3, unpack_body, [vmem], pltpu.HBM(fields_in.shape, BF16),
        [pltpu.VMEM(fields_in.shape, BF16)], ends, sems=rows_all, outs=hbm,
    )[None]

    def grad_call(flip):
        def body(*refs):
            grad_body(flip, *refs)

        return call(
            3, body, [smem] + [vmem] * 4, product, [], idx, coef0, coef1, grad0, grad1
        )

    got = lax.ppermute(grad_call(True), "section", swap)
    both = (grad_call(False).astype(F32) + got.astype(F32)).astype(BF16)

    def fold(value, axes, routes):
        step = value.shape[0] // 4
        total = 0.0
        for k, route in enumerate(routes):
            block = value[k * step : (k + 1) * step]
            if route is not None:
                block = lax.ppermute(block, axes, route)
            total += block.astype(F32)
        return total

    along = [None] + [[(i, (i + k) % 4) for i in range(4)] for k in range(1, 4)]
    across = []
    for k in range(4):
        across.append([])
        for z in range(4):
            for x in range(4):
                there = (z + k) % 4
                across[k].append((4 * z + x, 4 * there + (x if there < 2 else 3 - x)))
    total = fold(fold(both, "dp", along).astype(BF16), ("z", "x"), across)
    batch_count = rows_all * lax.axis_size("dp")
    return (section_ends, (total / batch_count)[None])


def solution(mesh):
    grid = Mesh(mesh.devices.reshape(2, 4, 4, 4), ("section", "z", "x", "dp"))
    rows = P("dp", ("z", "x"), None, None)
    in_specs = (rows, rows, P("section", None, None, None))
    out_specs = (
        P("section", "dp", ("z", "x"), None, None),
        P("section", ("z", "x", "dp"), None, None),
    )
    ta, ts = polar_tables(64, 4)

    def body(fields_in, cotangent, weights):
        return local(jnp.asarray(ta), jnp.asarray(ts), fields_in, cotangent, weights)

    return jax.shard_map(body, mesh=grid, in_specs=in_specs, out_specs=out_specs, check_vma=False)
```

```python
import math

import jax
import jax.numpy as jnp
import ml_dtypes
import numpy as np
from jax import lax
from jax.experimental import pallas as pl
from jax.experimental.pallas import tpu as pltpu
from jax.sharding import Mesh
from jax.sharding import PartitionSpec as P

BF16 = jnp.bfloat16
F32 = jnp.float32


def gauss_nodes(resolution):
    counter = np.arange(resolution) * 1.0
    guesses = np.cos(math.pi * (counter + 0.75) / (resolution + 0.5))
    for sweep in range(100):
        current = np.ones(resolution)
        previous = np.zeros(resolution)
        for degree in range(1, resolution + 1):
            following = (
                (2.0 * degree - 1.0) * guesses * current - (degree - 1.0) * previous
            ) / degree
            previous = current
            current = following
        slope_val = resolution * (guesses * current - previous) / (guesses * guesses - 1.0)
        guesses = guesses - current / slope_val
    current = np.ones(resolution)
    previous = np.zeros(resolution)
    for degree in range(1, resolution + 1):
        following = ((2.0 * degree - 1.0) * guesses * current - (degree - 1.0) * previous) / degree
        previous = current
        current = following
    slope_val = resolution * (guesses * current - previous) / (guesses * guesses - 1.0)
    weights_q = 2.0 / ((1.0 - guesses * guesses) * slope_val * slope_val)
    return (guesses[::-1].copy(), weights_q[::-1].copy())


def legendre_table(resolution):
    points, quadrature = gauss_nodes(resolution)
    sine_row = np.sqrt(1.0 - points * points)
    basis = np.zeros((resolution, resolution, resolution))
    diagonal = np.full(resolution, math.sqrt(1.0 / (4.0 * math.pi)))
    for harmonic in range(resolution):
        if harmonic > 0:
            diagonal = diagonal * sine_row * math.sqrt((2.0 * harmonic + 1.0) / (2.0 * harmonic))
        basis[harmonic, harmonic] = diagonal
        if harmonic + 1 < resolution:
            basis[harmonic, harmonic + 1] = points * math.sqrt(2.0 * harmonic + 3.0) * diagonal
        for degree in range(harmonic + 2, resolution):
            alpha_coef = math.sqrt(
                (4.0 * degree * degree - 1.0) / (degree * degree - harmonic * harmonic)
            )
            beta_coef = math.sqrt(
                ((degree - 1.0) ** 2 - harmonic * harmonic) / (4.0 * (degree - 1.0) ** 2 - 1.0)
            )
            basis[harmonic, degree] = alpha_coef * (
                points * basis[harmonic, degree - 1] - beta_coef * basis[harmonic, degree - 2]
            )
    return basis * np.sqrt(2.0 * math.pi * quadrature)[None, None, :]


def longitude_table(longitudes, degrees):
    column = np.arange(2 * degrees)
    harmonic, parity = column // 2, column % 2
    phase = (np.arange(longitudes)[:, None] * harmonic[None, :]) % longitudes
    angles = phase.astype(np.float32) * np.float32(2.0 * math.pi / longitudes)
    scales = np.where(harmonic == 0, 1.0 / math.sqrt(longitudes), math.sqrt(2.0 / longitudes))
    basis = np.where(parity[None, :] == 0, np.cos(angles), -np.sin(angles))
    return (basis * scales[None, :].astype(np.float32)).astype(ml_dtypes.bfloat16)


SLOTS = 72


def pair_degrees(degrees, blocks):
    quarter = degrees // 16
    return np.array(
        [
            16 * (r // quarter) + quarter * x + r % quarter
            for x in range(blocks)
            for r in range(degrees // 2 // blocks)
        ]
    )


def polar_tables(degrees, blocks):
    leg = legendre_table(degrees).astype(np.float32).astype(ml_dtypes.bfloat16)
    low = pair_degrees(degrees, blocks)
    pairs = degrees // 2
    ana = np.zeros((degrees + 1, 2, pairs, 2, pairs), ml_dtypes.bfloat16)
    syn = np.zeros((degrees, 2, pairs, 2, pairs), ml_dtypes.bfloat16)
    for half in range(2):
        for g, l in enumerate(low):
            for pos in range(degrees + 1):
                if l >= pos:
                    ana[pos, half, g, 1] = leg[pos, l, half::2]
                else:
                    ana[pos, half, g, 0] = leg[degrees - pos, degrees - 1 - l, half::2]
            for m in range(degrees):
                if l >= m:
                    syn[m, half, :, 1, g] = leg[m, l, half::2]
                if degrees - 1 - l >= m:
                    syn[m, half, :, 0, g] = leg[m, degrees - 1 - l, half::2]
    size = (2 * pairs, 2 * pairs)
    return ana.reshape((degrees + 1,) + size), syn.reshape((degrees,) + size)


def params(megabytes=16):
    return pltpu.CompilerParams(vmem_limit_bytes=megabytes * 2**20)


def cost(microseconds):
    return pl.CostEstimate(
        flops=int(microseconds * 1.1e9), bytes_accessed=1 << 20, transcendentals=0
    )


def dot(left, right):
    return jnp.dot(left, right, preferred_element_type=F32)


def normal_cdf(values):
    return 0.5 * (1.0 + lax.erf(values * (1.0 / math.sqrt(2.0))))


def low_lanes(shape):
    return lax.broadcasted_iota(jnp.int32, shape, len(shape) - 1) < shape[-1] // 2


def turned(value):
    return pltpu.roll(value, value.shape[-1] // 2, value.ndim - 1)


def interleave(first, second):
    low = low_lanes(first.shape)
    return jnp.where(low, first, turned(second)), jnp.where(low, turned(first), second)


def begin(source, target, sem):
    copy = pltpu.make_async_copy(source, target, sem)
    copy.start()
    return copy


def pack_body(idx_ref, field_hbm, cot_hbm, out_hbm, field_ref, cot_ref, out_ref, sem):
    samples, rows, _, channels = field_ref.shape
    loads, saves = [], []
    for s in range(samples):
        at = s + samples * idx_ref[1]
        loads.append(begin(field_hbm.at[at], field_ref.at[s], sem.at[s]))
        loads.append(begin(cot_hbm.at[at], cot_ref.at[s], sem.at[samples + s]))
    for s in range(samples):
        for i, ref in enumerate((field_ref, cot_ref)):
            loads[2 * s + i].wait()
            for q in range(rows // 2):
                for t in range(channels // 128):
                    span = slice(t * 128, (t + 1) * 128)
                    one, two = ref[s, 2 * q, :, span], ref[s, 2 * q + 1, :, span]
                    left, right = interleave(one.astype(F32), two.astype(F32))
                    out_ref[4 * s + 2 * t, i, q] = left.astype(BF16)
                    out_ref[4 * s + 2 * t + 1, i, q] = right.astype(BF16)
        span = pl.ds(4 * s, 4)
        saves.append(begin(out_ref.at[span], out_hbm.at[span], sem.at[2 * samples + s]))
    for save in saves:
        save.wait()


def unpack_body(in_ref, out_hbm, out_ref, sem):
    samples, rows, _, channels = out_ref.shape
    saves = []
    for s in range(samples):
        for q in range(rows // 2):
            for t in range(channels // 128):
                span = slice(t * 128, (t + 1) * 128)
                one, two = in_ref[4 * s + 2 * t, q], in_ref[4 * s + 2 * t + 1, q]
                one, two = interleave(one.astype(F32), two.astype(F32))
                out_ref[s, 2 * q, :, span] = one.astype(BF16)
                out_ref[s, 2 * q + 1, :, span] = two.astype(BF16)
        saves.append(begin(out_ref.at[s], out_hbm.at[s], sem.at[s]))
    for save in saves:
        save.wait()


def prepare_body(idx_ref, own_hbm, far_hbm, ta_hbm, ts_hbm, w0_ref, w1_ref, ta_ref, ts_ref, sem):
    quarter = w0_ref.shape[1] // 2

    def fetch(source, target, layer):
        copies = []
        for z in range(4):
            at = 4 * quarter * z + quarter * (idx_ref[0] if z < 2 else 3 - idx_ref[0])
            part = target.at[z // 2, pl.ds((z % 2) * quarter, quarter)]
            origin = source.at[0, pl.ds(at, quarter)]
            copies.append(pltpu.make_async_copy(origin, part, sem.at[4 * layer + z]))
        return copies

    tables = [begin(ta_hbm, ta_ref, sem.at[8]), begin(ts_hbm, ts_ref, sem.at[9])]
    front = idx_ref[1] == 0

    @pl.when(front)
    def _():
        for copy in fetch(own_hbm, w0_ref, 0) + fetch(far_hbm, w1_ref, 1):
            copy.start()

    @pl.when(jnp.logical_not(front))
    def _():
        for copy in fetch(far_hbm, w0_ref, 0) + fetch(own_hbm, w1_ref, 1):
            copy.start()

    for copy in fetch(own_hbm, w0_ref, 0) + fetch(own_hbm, w1_ref, 1) + tables:
        copy.wait()


def store_spectrum(q, value, spec_ref):
    spec_ref[pl.ds(q, 128, stride=32), :] = value


def spectrum_at(q, grid_ref):
    return grid_ref[q * 128 : (q + 1) * 128, :].astype(BF16)


def analyse(spec_ref, table_ref, slot_ref, out_ref):
    degrees = table_ref.shape[0] - 1
    pairs = degrees // 2

    low = low_lanes((pairs, 128))

    def order(m):
        rows = spec_ref[m * 2 * pairs : (m + 1) * 2 * pairs, :].astype(BF16)
        return jnp.concatenate([rows[:pairs], rows[pairs:]], axis=1)

    for pos in range(degrees + 1):
        right, left = order(min(degrees - pos, degrees - 1)), table_ref[pos]
        if pos < pairs:
            right = jnp.concatenate([right, order(pos)], axis=0)
        else:
            left = left[:, :pairs]
        both = dot(left, right)
        even, odd = both[:pairs], both[pairs:]
        value = jnp.where(low, even[:, :128], odd[:, 128:]) + turned(
            jnp.where(low, even[:, 128:], odd[:, :128])
        )
        slot_ref[pl.ds(pos, pairs, stride=SLOTS), :] = value
    for pos in range(degrees + 1, SLOTS):
        slot_ref[pl.ds(pos, pairs, stride=SLOTS), :] = jnp.zeros((pairs, 128), F32)
    blocks, rows, _ = out_ref.shape
    for b in range(blocks):
        out_ref[b] = slot_ref[b * rows : (b + 1) * rows, :].astype(BF16)


def synthesise(in_ref, table_ref, slot_ref, grid_ref):
    degrees = table_ref.shape[0]
    pairs = degrees // 2
    blocks, rows, _ = in_ref.shape
    for b in range(blocks):
        slot_ref[b * rows : (b + 1) * rows, :] = in_ref[b].astype(F32)

    for m in range(degrees):
        right = slot_ref[pl.ds(degrees - m, pairs, stride=SLOTS), :]
        left = table_ref[m]
        if m < pairs:
            low = slot_ref[pl.ds(m, pairs, stride=SLOTS), :]
            right = jnp.concatenate([right, low], axis=0)
        else:
            left = left[:, :pairs]
        both = dot(left, right.astype(BF16))
        real, imag = interleave(both[:pairs], both[pairs:])
        grid_ref[pl.ds(2 * m, pairs, stride=2 * degrees), :] = real
        grid_ref[pl.ds(2 * m + 1, pairs, stride=2 * degrees), :] = imag


def gelu_parts(pre):
    cdf = normal_cdf(pre)
    density = jnp.exp(-0.5 * pre * pre) * (1.0 / math.sqrt(2.0 * math.pi))
    return pre * cdf, cdf + pre * density


def beside(first, second):
    return jnp.concatenate([first, second], axis=1)


def spectra_at(d, grid_ref):
    return beside(spectrum_at(2 * d, grid_ref), spectrum_at(2 * d + 1, grid_ref))


def store_spectra(d, value, spec_ref):
    for q in range(2):
        store_spectrum(2 * d + q, value[:, q * 128 : (q + 1) * 128], spec_ref)


def first_body(recv_ref, ana_ref, ta_ref, out_ref, spec_ref, slot_ref):
    basis = ana_ref[...]
    for d in range(recv_ref.shape[0]):
        field = beside(recv_ref[d, 0, 0], recv_ref[d, 0, 1])
        store_spectra(d, dot(basis, field), spec_ref)
    analyse(spec_ref, ta_ref, slot_ref, out_ref)


def layer0_body(in_ref, recv_ref, syn_ref, ana_ref, ts_ref, ta_ref, h_ref, slope_ref, out_ref,
                spec_ref, grid_ref, slot_ref):
    synthesise(in_ref, ts_ref, slot_ref, grid_ref)
    syn, ana = syn_ref[...], ana_ref[...]
    for d in range(recv_ref.shape[0]):
        pre = dot(syn, spectra_at(d, grid_ref))
        made = []
        for q in range(2):
            value, slope = gelu_parts(pre[:, q * 128 : (q + 1) * 128])
            slope_ref[d, q] = slope.astype(BF16)
            h = (recv_ref[d, 0, q].astype(F32) + value).astype(BF16)
            h_ref[d, q] = h
            made.append(h)
        store_spectra(d, dot(ana, beside(*made)), spec_ref)
    analyse(spec_ref, ta_ref, slot_ref, out_ref)


def layer1_body(in_ref, recv_ref, h_ref, syn_ref, ana_ref, ts_ref, ta_ref, top_ref, out_ref,
                spec_ref, grid_ref, slot_ref):
    synthesise(in_ref, ts_ref, slot_ref, grid_ref)
    syn, ana = syn_ref[...], ana_ref[...]
    for d in range(recv_ref.shape[0]):
        pre = dot(syn, spectra_at(d, grid_ref))
        made = []
        for q in range(2):
            value, slope = gelu_parts(pre[:, q * 128 : (q + 1) * 128])
            top_ref[d, q] = (h_ref[d, q].astype(F32) + value).astype(BF16)
            made.append((recv_ref[d, 1, q].astype(F32) * slope).astype(BF16))
        store_spectra(d, dot(ana, beside(*made)), spec_ref)
    analyse(spec_ref, ta_ref, slot_ref, out_ref)


def back1_body(in_ref, recv_ref, slope_ref, syn_ref, ana_ref, ts_ref, ta_ref, g_ref, out_ref,
               spec_ref, grid_ref, slot_ref):
    synthesise(in_ref, ts_ref, slot_ref, grid_ref)
    syn, ana = syn_ref[...], ana_ref[...]
    for d in range(recv_ref.shape[0]):
        back = dot(syn, spectra_at(d, grid_ref))
        made = []
        for q in range(2):
            g = (recv_ref[d, 1, q].astype(F32) + back[:, q * 128 : (q + 1) * 128]).astype(BF16)
            g_ref[d, q] = g
            made.append((g.astype(F32) * slope_ref[d, q].astype(F32)).astype(BF16))
        store_spectra(d, dot(ana, beside(*made)), spec_ref)
    analyse(spec_ref, ta_ref, slot_ref, out_ref)


def back0_body(in_ref, g_ref, top_ref, syn_ref, ts_ref, ends_ref, grid_ref, slot_ref, sem):
    move = begin(top_ref, ends_ref.at[1], sem.at[0])
    synthesise(in_ref, ts_ref, slot_ref, grid_ref)
    syn = syn_ref[...]
    for d in range(g_ref.shape[0]):
        back = dot(syn, spectra_at(d, grid_ref))
        for q in range(2):
            part = back[:, q * 128 : (q + 1) * 128]
            ends_ref[0, d, q] = (g_ref[d, q].astype(F32) + part).astype(BF16)
    move.wait()


def lower_rows(x_at, r):
    index = lax.broadcasted_iota(jnp.int32, (2 * SLOTS, 256), 0)
    pos = jnp.where(index < SLOTS, index, index - SLOTS)
    return pos <= 16 * (r // 4) + r % 4 + 4 * x_at


def mix_body(backward, idx_ref, in_ref, w_ref, out_ref, coef_ref):
    pairs = w_ref.shape[1]
    contract = (((1,), (1 if backward else 0,)), ((), ()))
    rows = 2 * SLOTS
    for rr in range(pairs // 2):
        span = slice(rr * rows, (rr + 1) * rows)
        blocks = [in_ref[b, span].astype(F32) for b in range(4)]
        a0, a1 = interleave(blocks[0], blocks[1])
        b0, b1 = interleave(blocks[2], blocks[3])
        real = jnp.concatenate([a0, b0], axis=1)
        imag = jnp.concatenate([a1, b1], axis=1)
        reals, imags = [], []
        for r in (2 * rr, 2 * rr + 1):
            part = slice((r % 2) * SLOTS, (r % 2 + 1) * SLOTS)
            stack = jnp.concatenate([real[part], imag[part]], axis=0).astype(BF16)
            coef_ref[r] = stack
            one = lax.dot_general(stack, w_ref[0, r], contract, preferred_element_type=F32)
            two = lax.dot_general(
                stack, w_ref[1, pairs - 1 - r], contract, preferred_element_type=F32
            )
            mixed = jnp.where(lower_rows(idx_ref[0], r), one, two)
            reals.append(mixed[:SLOTS])
            imags.append(mixed[SLOTS:])
        real = jnp.concatenate(reals, axis=0)
        imag = jnp.concatenate(imags, axis=0)
        for t in range(2):
            lanes = slice(t * 128, (t + 1) * 128)
            left, right = interleave(real[:, lanes], imag[:, lanes])
            out_ref[2 * t, span] = left.astype(BF16)
            out_ref[2 * t + 1, span] = right.astype(BF16)


def grad_body(idx_ref, coef_ref, grad_ref, out_ref):
    pairs = coef_ref.shape[0]
    over = (((0,), (0,)), ((), ()))
    for r in range(pairs):
        grad = grad_ref[r].astype(F32)
        lower = lower_rows(idx_ref[0], r)
        pieces = (jnp.where(lower, grad, 0.0), jnp.where(lower, 0.0, grad))
        for at, piece in zip((r, 2 * pairs - 1 - r), pieces):
            place = 4 * ((at % 4 + 4 - idx_ref[2]) % 4) + (at // 4 + 4 - idx_ref[3]) % 4
            made = lax.dot_general(
                coef_ref[r], piece.astype(BF16), over, preferred_element_type=F32
            )
            out_ref[place] = made.astype(BF16)


def add_body(first_ref, second_ref, *parts):
    for k, part_ref in enumerate(parts):
        for i in range(4):
            total = first_ref[4 * k + i].astype(F32) + second_ref[4 * k + i].astype(F32)
            part_ref[i] = total.astype(BF16)


def fold_body(idx_ref, *refs):
    parts = refs[8:]

    def write(first, second, third, fourth):
        for k, part_ref in enumerate(parts):
            total = first[k].astype(F32) + second[k].astype(F32)
            part_ref[0] = (total + third[k].astype(F32) + fourth[k].astype(F32)).astype(BF16)

    @pl.when(idx_ref[1] == 0)
    def _():
        write(*refs[:4])

    @pl.when(idx_ref[1] == 1)
    def _():
        write(*refs[4:8])


def mean_body(count, first, second, third, fourth, out_ref):
    total = first[...].astype(F32) + second[...].astype(F32)
    total += third[...].astype(F32) + fourth[...].astype(F32)
    out_ref[...] = total / count


def local(ta, ts, fields_in, cotangent, weights):
    rows_all, lat_rows, longitudes, channels = fields_in.shape
    degrees = longitudes // 2
    samples = rows_all // 2
    section = lax.axis_index("section")
    x_at, z_at, y_at = lax.axis_index("x"), lax.axis_index("z"), lax.axis_index("dp")
    idx = jnp.stack([x_at, section, y_at, z_at]).astype(jnp.int32)
    syn_np = longitude_table(longitudes, degrees)
    syn = jnp.asarray(syn_np)
    ana = jnp.asarray(np.ascontiguousarray(syn_np.T))
    swap = [(0, 1), (1, 0)]
    pairs = degrees // 2
    q_rows = lat_rows // 2

    vmem = pl.BlockSpec(memory_space=pltpu.VMEM)
    smem = pl.BlockSpec(memory_space=pltpu.SMEM)
    hbm = pl.BlockSpec(memory_space=pltpu.HBM)
    half_shape = (16, q_rows, longitudes, 128)
    half = pltpu.VMEM(half_shape, BF16)
    spec = pltpu.VMEM((4, pairs // 4 * SLOTS, 128), BF16)
    coef = pltpu.VMEM((pairs // 4, 2 * SLOTS, channels), BF16)
    product = pltpu.VMEM((degrees // 4, channels, channels), BF16)
    chosen = pltpu.VMEM((2, pairs // 4, channels, channels), BF16)
    tall = pltpu.VMEM((pairs * 128, 128), F32)
    slots = pltpu.VMEM((pairs * SLOTS, 128), F32)

    def far_away(array):
        return pltpu.with_memory_space_constraint(array, pltpu.HBM)

    def near(array):
        return pltpu.with_memory_space_constraint(array, pltpu.VMEM)

    def call(time, body, ins, shapes, scratches, *args, sems=0, outs=None):
        many = isinstance(shapes, list)
        return pl.pallas_call(
            body,
            in_specs=ins,
            out_specs=outs or ([vmem] * len(shapes) if many else vmem),
            out_shape=shapes,
            scratch_shapes=scratches + [pltpu.SemaphoreType.DMA((sems,))] * (sems > 0),
            cost_estimate=cost(time),
            compiler_params=params(),
        )(*args)

    quarter_field = pltpu.VMEM((samples, lat_rows, longitudes, channels), BF16)
    packed = call(
        3, pack_body, [smem, hbm, hbm], pltpu.HBM((16, 2) + half_shape[1:], BF16),
        [quarter_field] * 2 + [pltpu.VMEM((16, 2) + half_shape[1:], BF16)],
        idx, far_away(fields_in), far_away(cotangent), sems=3 * samples, outs=hbm,
    )
    far = lax.ppermute(weights, "section", swap)
    w0, w1, ta, ts = call(
        2, prepare_body, [smem] + [hbm] * 4,
        [chosen, chosen, pltpu.VMEM(ta.shape, BF16), pltpu.VMEM(ts.shape, BF16)], [],
        idx, far_away(weights), far_away(far), far_away(ta), far_away(ts), sems=10,
    )
    recv = near(lax.all_to_all(packed, ("z", "x"), 0, 0, tiled=True))

    def turn(value):
        return near(lax.all_to_all(value, "x", 0, 0, tiled=True))

    def mix_call(value, weight, backward):
        def body(*refs):
            mix_body(backward, *refs)

        return call(2, body, [smem, vmem, vmem], [spec, coef], [], idx, value, weight)

    row = pltpu.VMEM((4, channels, channels), BF16)
    single = pltpu.VMEM((1, channels, channels), BF16)

    def exchange(parts, axes, routes):
        return [
            part if route is None else near(lax.ppermute(part, axes, route))
            for part, route in zip(parts, routes)
        ]

    def along_dp(first, second, layer):
        made = call(3, grad_body, [smem, vmem, vmem], product, [], idx, first, second)
        got = near(lax.ppermute(made, "section", [(1 - layer, layer)]))
        parts = call(2, add_body, [vmem] * 2, [row] * 4, [], made, got)
        routes = [None]
        for k in range(1, 4):
            routes.append([(4 * layer + i, 4 * layer + (i + k) % 4) for i in range(4)])
        return exchange(parts, ("section", "dp"), routes)

    def together(value, others):
        value, *others = lax.optimization_barrier((value, *others))
        return near(value), [near(other) for other in others]

    value = call(3, first_body, [vmem] * 3, spec, [tall, slots], recv, ana, ta)
    value, coef0 = mix_call(turn(value), w0, False)
    h1, slope, value = call(
        6, layer0_body, [vmem] * 6, [half, half, spec], [tall, tall, slots],
        turn(value), recv, syn, ana, ts, ta,
    )
    value, coef1 = mix_call(turn(value), w1, False)
    top, value = call(
        6, layer1_body, [vmem] * 7, [half, spec], [tall, tall, slots],
        turn(value), recv, h1, syn, ana, ts, ta,
    )
    value, grad1 = mix_call(turn(value), w1, True)
    g1, value = call(
        5, back1_body, [vmem] * 7, [half, spec], [tall, tall, slots],
        turn(value), recv, slope, syn, ana, ts, ta,
    )
    value, grad0 = mix_call(turn(value), w0, True)
    grad0, parts1 = together(grad0, along_dp(coef1, grad1, 1))
    value = turn(value)
    ends = call(
        4, back0_body, [vmem] * 5, pltpu.VMEM((2,) + half_shape, BF16), [tall, slots],
        value, g1, top, syn, ts, sems=1,
    )
    ends = ends.reshape((32,) + half_shape[1:])
    ends = near(lax.all_to_all(ends, ("section", "z", "x"), 0, 0, tiled=True))
    section_ends = call(
        3, unpack_body, [vmem], pltpu.HBM(fields_in.shape, BF16),
        [pltpu.VMEM(fields_in.shape, BF16)], ends, sems=rows_all, outs=hbm,
    )[None]

    across = []
    for k in range(4):
        across.append([])
        for z in range(4):
            for x in range(4):
                there = (z + k) % 4
                across[k].append((4 * z + x, 4 * there + (x if there < 2 else 3 - x)))
    parts0 = along_dp(coef0, grad0, 0)
    parts = call(2, fold_body, [smem] + [vmem] * 8, [single] * 4, [], idx, *parts0, *parts1)
    parts = exchange(parts, ("z", "x"), across)
    batch_count = rows_all * lax.axis_size("dp")

    def mean(*refs):
        mean_body(batch_count, *refs)

    total = call(1, mean, [vmem] * 4, jax.ShapeDtypeStruct(single.shape, F32), [], *parts)
    return (section_ends, total[None])


def solution(mesh):
    grid = Mesh(mesh.devices.reshape(2, 4, 4, 4), ("section", "z", "x", "dp"))
    rows = P("dp", ("z", "x"), None, None)
    in_specs = (rows, rows, P("section", None, None, None))
    out_specs = (
        P("section", "dp", ("z", "x"), None, None),
        P("section", ("z", "x", "dp"), None, None),
    )
    ta, ts = polar_tables(64, 4)

    def body(fields_in, cotangent, weights):
        return local(jnp.asarray(ta), jnp.asarray(ts), fields_in, cotangent, weights)

    return jax.shard_map(body, mesh=grid, in_specs=in_specs, out_specs=out_specs, check_vma=False)
```

```python
import math

import jax
import jax.numpy as jnp
import ml_dtypes
import numpy as np
from jax import lax
from jax.experimental import pallas as pl
from jax.experimental.pallas import tpu as pltpu
from jax.sharding import Mesh
from jax.sharding import PartitionSpec as P

BF16 = jnp.bfloat16
F32 = jnp.float32


def gauss_nodes(resolution):
    counter = np.arange(resolution) * 1.0
    guesses = np.cos(math.pi * (counter + 0.75) / (resolution + 0.5))
    for sweep in range(100):
        current = np.ones(resolution)
        previous = np.zeros(resolution)
        for degree in range(1, resolution + 1):
            following = (
                (2.0 * degree - 1.0) * guesses * current - (degree - 1.0) * previous
            ) / degree
            previous = current
            current = following
        slope_val = resolution * (guesses * current - previous) / (guesses * guesses - 1.0)
        guesses = guesses - current / slope_val
    current = np.ones(resolution)
    previous = np.zeros(resolution)
    for degree in range(1, resolution + 1):
        following = ((2.0 * degree - 1.0) * guesses * current - (degree - 1.0) * previous) / degree
        previous = current
        current = following
    slope_val = resolution * (guesses * current - previous) / (guesses * guesses - 1.0)
    weights_q = 2.0 / ((1.0 - guesses * guesses) * slope_val * slope_val)
    return (guesses[::-1].copy(), weights_q[::-1].copy())


def legendre_table(resolution):
    points, quadrature = gauss_nodes(resolution)
    sine_row = np.sqrt(1.0 - points * points)
    basis = np.zeros((resolution, resolution, resolution))
    diagonal = np.full(resolution, math.sqrt(1.0 / (4.0 * math.pi)))
    for harmonic in range(resolution):
        if harmonic > 0:
            diagonal = diagonal * sine_row * math.sqrt((2.0 * harmonic + 1.0) / (2.0 * harmonic))
        basis[harmonic, harmonic] = diagonal
        if harmonic + 1 < resolution:
            basis[harmonic, harmonic + 1] = points * math.sqrt(2.0 * harmonic + 3.0) * diagonal
        for degree in range(harmonic + 2, resolution):
            alpha_coef = math.sqrt(
                (4.0 * degree * degree - 1.0) / (degree * degree - harmonic * harmonic)
            )
            beta_coef = math.sqrt(
                ((degree - 1.0) ** 2 - harmonic * harmonic) / (4.0 * (degree - 1.0) ** 2 - 1.0)
            )
            basis[harmonic, degree] = alpha_coef * (
                points * basis[harmonic, degree - 1] - beta_coef * basis[harmonic, degree - 2]
            )
    return basis * np.sqrt(2.0 * math.pi * quadrature)[None, None, :]


def longitude_table(longitudes, degrees):
    column = np.arange(2 * degrees)
    harmonic, parity = column // 2, column % 2
    phase = (np.arange(longitudes)[:, None] * harmonic[None, :]) % longitudes
    angles = phase.astype(np.float32) * np.float32(2.0 * math.pi / longitudes)
    scales = np.where(harmonic == 0, 1.0 / math.sqrt(longitudes), math.sqrt(2.0 / longitudes))
    basis = np.where(parity[None, :] == 0, np.cos(angles), -np.sin(angles))
    return (basis * scales[None, :].astype(np.float32)).astype(ml_dtypes.bfloat16)


SLOTS = 72


def pair_degrees(degrees, blocks):
    quarter = degrees // 16
    return np.array(
        [
            16 * (r // quarter) + quarter * x + r % quarter
            for x in range(blocks)
            for r in range(degrees // 2 // blocks)
        ]
    )


def polar_tables(degrees, blocks):
    leg = legendre_table(degrees).astype(np.float32).astype(ml_dtypes.bfloat16)
    low = pair_degrees(degrees, blocks)
    pairs = degrees // 2
    ana = np.zeros((degrees + 1, 2, pairs, 2, pairs), ml_dtypes.bfloat16)
    syn = np.zeros((degrees, 2, pairs, 2, pairs), ml_dtypes.bfloat16)
    for half in range(2):
        for g, l in enumerate(low):
            for pos in range(degrees + 1):
                if l >= pos:
                    ana[pos, half, g, 1] = leg[pos, l, half::2]
                else:
                    ana[pos, half, g, 0] = leg[degrees - pos, degrees - 1 - l, half::2]
            for m in range(degrees):
                if l >= m:
                    syn[m, half, :, 1, g] = leg[m, l, half::2]
                if degrees - 1 - l >= m:
                    syn[m, half, :, 0, g] = leg[m, degrees - 1 - l, half::2]
    size = (2 * pairs, 2 * pairs)
    return ana.reshape((degrees + 1,) + size), syn.reshape((degrees,) + size)


def params(megabytes=16):
    return pltpu.CompilerParams(vmem_limit_bytes=megabytes * 2**20)


def cost(microseconds):
    return pl.CostEstimate(
        flops=int(microseconds * 1.1e9), bytes_accessed=1 << 20, transcendentals=0
    )


def dot(left, right):
    return jnp.dot(left, right, preferred_element_type=F32)


def normal_cdf(values):
    return 0.5 * (1.0 + lax.erf(values * (1.0 / math.sqrt(2.0))))


def low_lanes(shape):
    return lax.broadcasted_iota(jnp.int32, shape, len(shape) - 1) < shape[-1] // 2


def turned(value):
    return pltpu.roll(value, value.shape[-1] // 2, value.ndim - 1)


def interleave(first, second):
    low = low_lanes(first.shape)
    return jnp.where(low, first, turned(second)), jnp.where(low, turned(first), second)


def begin(source, target, sem):
    copy = pltpu.make_async_copy(source, target, sem)
    copy.start()
    return copy


def pack_body(idx_ref, field_hbm, cot_hbm, out_hbm, field_ref, cot_ref, out_ref, sem):
    samples, rows, _, channels = field_ref.shape
    loads, saves = [], []
    for s in range(samples):
        at = s + samples * idx_ref[1]
        loads.append(begin(field_hbm.at[at], field_ref.at[s], sem.at[s]))
        loads.append(begin(cot_hbm.at[at], cot_ref.at[s], sem.at[samples + s]))
    for s in range(samples):
        for i, ref in enumerate((field_ref, cot_ref)):
            loads[2 * s + i].wait()
            for q in range(rows // 2):
                for t in range(channels // 128):
                    span = slice(t * 128, (t + 1) * 128)
                    one, two = ref[s, 2 * q, :, span], ref[s, 2 * q + 1, :, span]
                    left, right = interleave(one.astype(F32), two.astype(F32))
                    out_ref[4 * s + 2 * t, i, q] = left.astype(BF16)
                    out_ref[4 * s + 2 * t + 1, i, q] = right.astype(BF16)
        span = pl.ds(4 * s, 4)
        saves.append(begin(out_ref.at[span], out_hbm.at[span], sem.at[2 * samples + s]))
    for save in saves:
        save.wait()


def unpack_body(in_ref, out_hbm, out_ref, sem):
    samples, rows, _, channels = out_ref.shape
    saves = []
    for s in range(samples):
        for q in range(rows // 2):
            for t in range(channels // 128):
                span = slice(t * 128, (t + 1) * 128)
                one, two = in_ref[4 * s + 2 * t, q], in_ref[4 * s + 2 * t + 1, q]
                one, two = interleave(one.astype(F32), two.astype(F32))
                out_ref[s, 2 * q, :, span] = one.astype(BF16)
                out_ref[s, 2 * q + 1, :, span] = two.astype(BF16)
        saves.append(begin(out_ref.at[s], out_hbm.at[s], sem.at[s]))
    for save in saves:
        save.wait()


def prepare_body(idx_ref, own_hbm, far_hbm, ta_hbm, ts_hbm, w0_ref, w1_ref, ta_ref, ts_ref, sem):
    quarter = w0_ref.shape[1] // 2

    def fetch(source, target, layer):
        copies = []
        for z in range(4):
            at = 4 * quarter * z + quarter * (idx_ref[0] if z < 2 else 3 - idx_ref[0])
            part = target.at[z // 2, pl.ds((z % 2) * quarter, quarter)]
            origin = source.at[0, pl.ds(at, quarter)]
            copies.append(pltpu.make_async_copy(origin, part, sem.at[4 * layer + z]))
        return copies

    tables = [begin(ta_hbm, ta_ref, sem.at[8]), begin(ts_hbm, ts_ref, sem.at[9])]
    front = idx_ref[1] == 0

    @pl.when(front)
    def _():
        for copy in fetch(own_hbm, w0_ref, 0) + fetch(far_hbm, w1_ref, 1):
            copy.start()

    @pl.when(jnp.logical_not(front))
    def _():
        for copy in fetch(far_hbm, w0_ref, 0) + fetch(own_hbm, w1_ref, 1):
            copy.start()

    for copy in fetch(own_hbm, w0_ref, 0) + fetch(own_hbm, w1_ref, 1) + tables:
        copy.wait()


def store_spectrum(q, value, spec_ref):
    spec_ref[pl.ds(q, 128, stride=32), :] = value


def spectrum_at(q, grid_ref):
    return grid_ref[q * 128 : (q + 1) * 128, :].astype(BF16)


def analyse(spec_ref, table_ref, slot_ref, out_ref):
    degrees = table_ref.shape[0] - 1
    pairs = degrees // 2

    low = low_lanes((pairs, 128))

    def order(m):
        rows = spec_ref[m * 2 * pairs : (m + 1) * 2 * pairs, :].astype(BF16)
        return jnp.concatenate([rows[:pairs], rows[pairs:]], axis=1)

    for pos in range(degrees + 1):
        right, left = order(min(degrees - pos, degrees - 1)), table_ref[pos]
        if pos < pairs:
            right = jnp.concatenate([right, order(pos)], axis=0)
        else:
            left = left[:, :pairs]
        both = dot(left, right)
        even, odd = both[:pairs], both[pairs:]
        value = jnp.where(low, even[:, :128], odd[:, 128:]) + turned(
            jnp.where(low, even[:, 128:], odd[:, :128])
        )
        slot_ref[pl.ds(pos, pairs, stride=SLOTS), :] = value
    for pos in range(degrees + 1, SLOTS):
        slot_ref[pl.ds(pos, pairs, stride=SLOTS), :] = jnp.zeros((pairs, 128), F32)
    blocks, rows, _ = out_ref.shape
    for b in range(blocks):
        out_ref[b] = slot_ref[b * rows : (b + 1) * rows, :].astype(BF16)


def synthesise(in_ref, table_ref, slot_ref, grid_ref):
    degrees = table_ref.shape[0]
    pairs = degrees // 2
    blocks, rows, _ = in_ref.shape
    for b in range(blocks):
        slot_ref[b * rows : (b + 1) * rows, :] = in_ref[b].astype(F32)

    for m in range(degrees):
        right = slot_ref[pl.ds(degrees - m, pairs, stride=SLOTS), :]
        left = table_ref[m]
        if m < pairs:
            low = slot_ref[pl.ds(m, pairs, stride=SLOTS), :]
            right = jnp.concatenate([right, low], axis=0)
        else:
            left = left[:, :pairs]
        both = dot(left, right.astype(BF16))
        real, imag = interleave(both[:pairs], both[pairs:])
        grid_ref[pl.ds(2 * m, pairs, stride=2 * degrees), :] = real
        grid_ref[pl.ds(2 * m + 1, pairs, stride=2 * degrees), :] = imag


def gelu_parts(pre):
    cdf = normal_cdf(pre)
    density = jnp.exp(-0.5 * pre * pre) * (1.0 / math.sqrt(2.0 * math.pi))
    return pre * cdf, cdf + pre * density


def beside(first, second):
    return jnp.concatenate([first, second], axis=1)


def spectra_at(d, grid_ref):
    return beside(spectrum_at(2 * d, grid_ref), spectrum_at(2 * d + 1, grid_ref))


def store_spectra(d, value, spec_ref):
    for q in range(2):
        store_spectrum(2 * d + q, value[:, q * 128 : (q + 1) * 128], spec_ref)


def first_body(recv_ref, ana_ref, ta_ref, out_ref, spec_ref, slot_ref):
    basis = ana_ref[...]
    for d in range(recv_ref.shape[0]):
        field = beside(recv_ref[d, 0, 0], recv_ref[d, 0, 1])
        store_spectra(d, dot(basis, field), spec_ref)
    analyse(spec_ref, ta_ref, slot_ref, out_ref)


def layer0_body(in_ref, recv_ref, syn_ref, ana_ref, ts_ref, ta_ref, h_ref, slope_ref, out_ref,
                spec_ref, grid_ref, slot_ref):
    synthesise(in_ref, ts_ref, slot_ref, grid_ref)
    syn, ana = syn_ref[...], ana_ref[...]
    for d in range(recv_ref.shape[0]):
        pre = dot(syn, spectra_at(d, grid_ref))
        made = []
        for q in range(2):
            value, slope = gelu_parts(pre[:, q * 128 : (q + 1) * 128])
            slope_ref[d, q] = slope.astype(BF16)
            h = (recv_ref[d, 0, q].astype(F32) + value).astype(BF16)
            h_ref[d, q] = h
            made.append(h)
        store_spectra(d, dot(ana, beside(*made)), spec_ref)
    analyse(spec_ref, ta_ref, slot_ref, out_ref)


def layer1_body(in_ref, recv_ref, h_ref, syn_ref, ana_ref, ts_ref, ta_ref, top_ref, out_ref,
                spec_ref, grid_ref, slot_ref):
    synthesise(in_ref, ts_ref, slot_ref, grid_ref)
    syn, ana = syn_ref[...], ana_ref[...]
    for d in range(recv_ref.shape[0]):
        pre = dot(syn, spectra_at(d, grid_ref))
        made = []
        for q in range(2):
            value, slope = gelu_parts(pre[:, q * 128 : (q + 1) * 128])
            top_ref[d, q] = (h_ref[d, q].astype(F32) + value).astype(BF16)
            made.append((recv_ref[d, 1, q].astype(F32) * slope).astype(BF16))
        store_spectra(d, dot(ana, beside(*made)), spec_ref)
    analyse(spec_ref, ta_ref, slot_ref, out_ref)


def back1_body(in_ref, recv_ref, slope_ref, syn_ref, ana_ref, ts_ref, ta_ref, g_ref, out_ref,
               spec_ref, grid_ref, slot_ref):
    synthesise(in_ref, ts_ref, slot_ref, grid_ref)
    syn, ana = syn_ref[...], ana_ref[...]
    for d in range(recv_ref.shape[0]):
        back = dot(syn, spectra_at(d, grid_ref))
        made = []
        for q in range(2):
            g = (recv_ref[d, 1, q].astype(F32) + back[:, q * 128 : (q + 1) * 128]).astype(BF16)
            g_ref[d, q] = g
            made.append((g.astype(F32) * slope_ref[d, q].astype(F32)).astype(BF16))
        store_spectra(d, dot(ana, beside(*made)), spec_ref)
    analyse(spec_ref, ta_ref, slot_ref, out_ref)


def back0_body(in_ref, g_ref, top_ref, syn_ref, ts_ref, ends_ref, grid_ref, slot_ref, sem):
    move = begin(top_ref, ends_ref.at[1], sem.at[0])
    synthesise(in_ref, ts_ref, slot_ref, grid_ref)
    syn = syn_ref[...]
    for d in range(g_ref.shape[0]):
        back = dot(syn, spectra_at(d, grid_ref))
        for q in range(2):
            part = back[:, q * 128 : (q + 1) * 128]
            ends_ref[0, d, q] = (g_ref[d, q].astype(F32) + part).astype(BF16)
    move.wait()


def lower_rows(x_at, r):
    index = lax.broadcasted_iota(jnp.int32, (2 * SLOTS, 256), 0)
    pos = jnp.where(index < SLOTS, index, index - SLOTS)
    return pos <= 16 * (r // 4) + r % 4 + 4 * x_at


def mix_body(backward, idx_ref, in_ref, w_ref, out_ref, coef_ref):
    pairs = w_ref.shape[1]
    contract = (((1,), (1 if backward else 0,)), ((), ()))
    rows = 2 * SLOTS
    for rr in range(pairs // 2):
        span = slice(rr * rows, (rr + 1) * rows)
        blocks = [in_ref[b, span].astype(F32) for b in range(4)]
        a0, a1 = interleave(blocks[0], blocks[1])
        b0, b1 = interleave(blocks[2], blocks[3])
        real = jnp.concatenate([a0, b0], axis=1)
        imag = jnp.concatenate([a1, b1], axis=1)
        reals, imags = [], []
        for r in (2 * rr, 2 * rr + 1):
            part = slice((r % 2) * SLOTS, (r % 2 + 1) * SLOTS)
            stack = jnp.concatenate([real[part], imag[part]], axis=0).astype(BF16)
            coef_ref[r] = stack
            one = lax.dot_general(stack, w_ref[0, r], contract, preferred_element_type=F32)
            two = lax.dot_general(
                stack, w_ref[1, pairs - 1 - r], contract, preferred_element_type=F32
            )
            mixed = jnp.where(lower_rows(idx_ref[0], r), one, two)
            reals.append(mixed[:SLOTS])
            imags.append(mixed[SLOTS:])
        real = jnp.concatenate(reals, axis=0)
        imag = jnp.concatenate(imags, axis=0)
        for t in range(2):
            lanes = slice(t * 128, (t + 1) * 128)
            left, right = interleave(real[:, lanes], imag[:, lanes])
            out_ref[2 * t, span] = left.astype(BF16)
            out_ref[2 * t + 1, span] = right.astype(BF16)


def grad_body(idx_ref, coef_ref, grad_ref, out_ref):
    pairs = coef_ref.shape[0]
    over = (((0,), (0,)), ((), ()))
    for r in range(pairs):
        grad = grad_ref[r].astype(F32)
        lower = lower_rows(idx_ref[0], r)
        pieces = (jnp.where(lower, grad, 0.0), jnp.where(lower, 0.0, grad))
        for at, piece in zip((r, 2 * pairs - 1 - r), pieces):
            place = 4 * ((at % 4 + 4 - idx_ref[2]) % 4) + (at // 4 + 4 - idx_ref[3]) % 4
            made = lax.dot_general(
                coef_ref[r], piece.astype(BF16), over, preferred_element_type=F32
            )
            out_ref[place] = made.astype(BF16)


def add_body(first_ref, second_ref, *parts):
    for k, part_ref in enumerate(parts):
        for i in range(4):
            total = first_ref[4 * k + i].astype(F32) + second_ref[4 * k + i].astype(F32)
            part_ref[i] = total.astype(BF16)


def fold_body(idx_ref, *refs):
    parts = refs[8:]

    def write(first, second, third, fourth):
        for k, part_ref in enumerate(parts):
            total = first[k].astype(F32) + second[k].astype(F32)
            part_ref[0] = (total + third[k].astype(F32) + fourth[k].astype(F32)).astype(BF16)

    @pl.when(idx_ref[1] == 0)
    def _():
        write(*refs[:4])

    @pl.when(idx_ref[1] == 1)
    def _():
        write(*refs[4:8])


def mean_body(count, first, second, third, fourth, out_ref):
    total = first[...].astype(F32) + second[...].astype(F32)
    total += third[...].astype(F32) + fourth[...].astype(F32)
    out_ref[...] = total / count


def local(ta, ts, fields_in, cotangent, weights):
    rows_all, lat_rows, longitudes, channels = fields_in.shape
    degrees = longitudes // 2
    samples = rows_all // 2
    section = lax.axis_index("section")
    x_at, z_at, y_at = lax.axis_index("x"), lax.axis_index("z"), lax.axis_index("dp")
    idx = jnp.stack([x_at, section, y_at, z_at]).astype(jnp.int32)
    syn_np = longitude_table(longitudes, degrees)
    syn = jnp.asarray(syn_np)
    ana = jnp.asarray(np.ascontiguousarray(syn_np.T))
    swap = [(0, 1), (1, 0)]
    pairs = degrees // 2
    q_rows = lat_rows // 2

    vmem = pl.BlockSpec(memory_space=pltpu.VMEM)
    smem = pl.BlockSpec(memory_space=pltpu.SMEM)
    hbm = pl.BlockSpec(memory_space=pltpu.HBM)
    half_shape = (16, q_rows, longitudes, 128)
    half = pltpu.VMEM(half_shape, BF16)
    spec = pltpu.VMEM((4, pairs // 4 * SLOTS, 128), BF16)
    coef = pltpu.VMEM((pairs // 4, 2 * SLOTS, channels), BF16)
    product = pltpu.VMEM((degrees // 4, channels, channels), BF16)
    chosen = pltpu.VMEM((2, pairs // 4, channels, channels), BF16)
    tall = pltpu.VMEM((pairs * 128, 128), F32)
    slots = pltpu.VMEM((pairs * SLOTS, 128), F32)

    def far_away(array):
        return pltpu.with_memory_space_constraint(array, pltpu.HBM)

    def near(array):
        return pltpu.with_memory_space_constraint(array, pltpu.VMEM)

    def call(time, body, ins, shapes, scratches, *args, sems=0, outs=None):
        many = isinstance(shapes, list)
        return pl.pallas_call(
            body,
            in_specs=ins,
            out_specs=outs or ([vmem] * len(shapes) if many else vmem),
            out_shape=shapes,
            scratch_shapes=scratches + [pltpu.SemaphoreType.DMA((sems,))] * (sems > 0),
            cost_estimate=cost(time),
            compiler_params=params(),
        )(*args)

    quarter_field = pltpu.VMEM((samples, lat_rows, longitudes, channels), BF16)
    packed = call(
        3, pack_body, [smem, hbm, hbm], pltpu.HBM((16, 2) + half_shape[1:], BF16),
        [quarter_field] * 2 + [pltpu.VMEM((16, 2) + half_shape[1:], BF16)],
        idx, far_away(fields_in), far_away(cotangent), sems=3 * samples, outs=hbm,
    )
    far = lax.ppermute(weights, "section", swap)
    w0, w1, ta, ts = call(
        2, prepare_body, [smem] + [hbm] * 4,
        [chosen, chosen, pltpu.VMEM(ta.shape, BF16), pltpu.VMEM(ts.shape, BF16)], [],
        idx, far_away(weights), far_away(far), far_away(ta), far_away(ts), sems=10,
    )
    recv = near(lax.all_to_all(packed, ("z", "x"), 0, 0, tiled=True))

    def turn(value):
        return near(lax.all_to_all(value, "x", 0, 0, tiled=True))

    def mix_call(value, weight, backward):
        def body(*refs):
            mix_body(backward, *refs)

        return call(2, body, [smem, vmem, vmem], [spec, coef], [], idx, value, weight)

    row = pltpu.VMEM((4, channels, channels), BF16)
    single = pltpu.VMEM((1, channels, channels), BF16)

    def exchange(parts, axes, routes):
        return [
            part if route is None else near(lax.ppermute(part, axes, route))
            for part, route in zip(parts, routes)
        ]

    def along_dp(first, second, layer):
        made = call(3, grad_body, [smem, vmem, vmem], product, [], idx, first, second)
        got = near(lax.ppermute(made, "section", [(1 - layer, layer)]))
        parts = call(2, add_body, [vmem] * 2, [row] * 4, [], made, got)
        routes = [None]
        for k in range(1, 4):
            routes.append([(4 * layer + i, 4 * layer + (i + k) % 4) for i in range(4)])
        return exchange(parts, ("section", "dp"), routes)

    def together(value, others):
        value, *others = lax.optimization_barrier((value, *others))
        return near(value), [near(other) for other in others]

    value = call(3, first_body, [vmem] * 3, spec, [tall, slots], recv, ana, ta)
    value, coef0 = mix_call(turn(value), w0, False)
    h1, slope, value = call(
        6, layer0_body, [vmem] * 6, [half, half, spec], [tall, tall, slots],
        turn(value), recv, syn, ana, ts, ta,
    )
    value, coef1 = mix_call(turn(value), w1, False)
    top, value = call(
        6, layer1_body, [vmem] * 7, [half, spec], [tall, tall, slots],
        turn(value), recv, h1, syn, ana, ts, ta,
    )
    value, grad1 = mix_call(turn(value), w1, True)
    g1, value = call(
        5, back1_body, [vmem] * 7, [half, spec], [tall, tall, slots],
        turn(value), recv, slope, syn, ana, ts, ta,
    )
    value, grad0 = mix_call(turn(value), w0, True)
    parts1 = along_dp(coef1, grad1, 1)
    grad0, early = together(grad0, [parts1[k] for k in (0, 1, 3)])
    parts1 = [early[0], early[1], parts1[2], early[2]]
    value = turn(value)
    ends = call(
        4, back0_body, [vmem] * 5, pltpu.VMEM((2,) + half_shape, BF16), [tall, slots],
        value, g1, top, syn, ts, sems=1,
    )
    ends = ends.reshape((32,) + half_shape[1:])
    ends = near(lax.all_to_all(ends, ("section", "z", "x"), 0, 0, tiled=True))
    section_ends = call(
        3, unpack_body, [vmem], pltpu.HBM(fields_in.shape, BF16),
        [pltpu.VMEM(fields_in.shape, BF16)], ends, sems=rows_all, outs=hbm,
    )[None]

    across = []
    for k in range(4):
        across.append([])
        for z in range(4):
            for x in range(4):
                there = (z + k) % 4
                across[k].append((4 * z + x, 4 * there + (x if there < 2 else 3 - x)))
    parts0 = along_dp(coef0, grad0, 0)
    parts = call(2, fold_body, [smem] + [vmem] * 8, [single] * 4, [], idx, *parts0, *parts1)
    parts = exchange(parts, ("z", "x"), across)
    batch_count = rows_all * lax.axis_size("dp")

    def mean(*refs):
        mean_body(batch_count, *refs)

    total = call(1, mean, [vmem] * 4, jax.ShapeDtypeStruct(single.shape, F32), [], *parts)
    return (section_ends, total[None])


def solution(mesh):
    grid = Mesh(mesh.devices.reshape(2, 4, 4, 4), ("section", "z", "x", "dp"))
    rows = P("dp", ("z", "x"), None, None)
    in_specs = (rows, rows, P("section", None, None, None))
    out_specs = (
        P("section", "dp", ("z", "x"), None, None),
        P("section", ("z", "x", "dp"), None, None),
    )
    ta, ts = polar_tables(64, 4)

    def body(fields_in, cotangent, weights):
        return local(jnp.asarray(ta), jnp.asarray(ts), fields_in, cotangent, weights)

    return jax.shard_map(body, mesh=grid, in_specs=in_specs, out_specs=out_specs, check_vma=False)
```

```python
import math

import jax
import jax.numpy as jnp
import ml_dtypes
import numpy as np
from jax import lax
from jax.experimental import pallas as pl
from jax.experimental.pallas import tpu as pltpu
from jax.sharding import Mesh
from jax.sharding import PartitionSpec as P

BF16 = jnp.bfloat16
F32 = jnp.float32


def gauss_nodes(resolution):
    counter = np.arange(resolution) * 1.0
    guesses = np.cos(math.pi * (counter + 0.75) / (resolution + 0.5))
    for sweep in range(100):
        current = np.ones(resolution)
        previous = np.zeros(resolution)
        for degree in range(1, resolution + 1):
            following = (
                (2.0 * degree - 1.0) * guesses * current - (degree - 1.0) * previous
            ) / degree
            previous = current
            current = following
        slope_val = resolution * (guesses * current - previous) / (guesses * guesses - 1.0)
        guesses = guesses - current / slope_val
    current = np.ones(resolution)
    previous = np.zeros(resolution)
    for degree in range(1, resolution + 1):
        following = ((2.0 * degree - 1.0) * guesses * current - (degree - 1.0) * previous) / degree
        previous = current
        current = following
    slope_val = resolution * (guesses * current - previous) / (guesses * guesses - 1.0)
    weights_q = 2.0 / ((1.0 - guesses * guesses) * slope_val * slope_val)
    return (guesses[::-1].copy(), weights_q[::-1].copy())


def legendre_table(resolution):
    points, quadrature = gauss_nodes(resolution)
    sine_row = np.sqrt(1.0 - points * points)
    basis = np.zeros((resolution, resolution, resolution))
    diagonal = np.full(resolution, math.sqrt(1.0 / (4.0 * math.pi)))
    for harmonic in range(resolution):
        if harmonic > 0:
            diagonal = diagonal * sine_row * math.sqrt((2.0 * harmonic + 1.0) / (2.0 * harmonic))
        basis[harmonic, harmonic] = diagonal
        if harmonic + 1 < resolution:
            basis[harmonic, harmonic + 1] = points * math.sqrt(2.0 * harmonic + 3.0) * diagonal
        for degree in range(harmonic + 2, resolution):
            alpha_coef = math.sqrt(
                (4.0 * degree * degree - 1.0) / (degree * degree - harmonic * harmonic)
            )
            beta_coef = math.sqrt(
                ((degree - 1.0) ** 2 - harmonic * harmonic) / (4.0 * (degree - 1.0) ** 2 - 1.0)
            )
            basis[harmonic, degree] = alpha_coef * (
                points * basis[harmonic, degree - 1] - beta_coef * basis[harmonic, degree - 2]
            )
    return basis * np.sqrt(2.0 * math.pi * quadrature)[None, None, :]


def longitude_table(longitudes, degrees):
    column = np.arange(2 * degrees)
    harmonic, parity = column // 2, column % 2
    phase = (np.arange(longitudes)[:, None] * harmonic[None, :]) % longitudes
    angles = phase.astype(np.float32) * np.float32(2.0 * math.pi / longitudes)
    scales = np.where(harmonic == 0, 1.0 / math.sqrt(longitudes), math.sqrt(2.0 / longitudes))
    basis = np.where(parity[None, :] == 0, np.cos(angles), -np.sin(angles))
    return (basis * scales[None, :].astype(np.float32)).astype(ml_dtypes.bfloat16)


SLOTS = 72


def pair_degrees(degrees, blocks):
    quarter = degrees // 16
    return np.array(
        [
            16 * (r // quarter) + quarter * x + r % quarter
            for x in range(blocks)
            for r in range(degrees // 2 // blocks)
        ]
    )


def polar_tables(degrees, blocks):
    leg = legendre_table(degrees).astype(np.float32).astype(ml_dtypes.bfloat16)
    low = pair_degrees(degrees, blocks)
    pairs = degrees // 2
    ana = np.zeros((degrees + 1, 2, pairs, 2, pairs), ml_dtypes.bfloat16)
    syn = np.zeros((degrees, 2, pairs, 2, pairs), ml_dtypes.bfloat16)
    for half in range(2):
        for g, l in enumerate(low):
            for pos in range(degrees + 1):
                if l >= pos:
                    ana[pos, half, g, 1] = leg[pos, l, half::2]
                else:
                    ana[pos, half, g, 0] = leg[degrees - pos, degrees - 1 - l, half::2]
            for m in range(degrees):
                if l >= m:
                    syn[m, half, :, 1, g] = leg[m, l, half::2]
                if degrees - 1 - l >= m:
                    syn[m, half, :, 0, g] = leg[m, degrees - 1 - l, half::2]
    size = (2 * pairs, 2 * pairs)
    return ana.reshape((degrees + 1,) + size), syn.reshape((degrees,) + size)


def params(megabytes=16):
    return pltpu.CompilerParams(vmem_limit_bytes=megabytes * 2**20)


def cost(microseconds):
    return pl.CostEstimate(
        flops=int(microseconds * 1.1e9), bytes_accessed=1 << 20, transcendentals=0
    )


def dot(left, right):
    return jnp.dot(left, right, preferred_element_type=F32)


def normal_cdf(values):
    return 0.5 * (1.0 + lax.erf(values * (1.0 / math.sqrt(2.0))))


def low_lanes(shape):
    return lax.broadcasted_iota(jnp.int32, shape, len(shape) - 1) < shape[-1] // 2


def turned(value):
    return pltpu.roll(value, value.shape[-1] // 2, value.ndim - 1)


def interleave(first, second):
    low = low_lanes(first.shape)
    return jnp.where(low, first, turned(second)), jnp.where(low, turned(first), second)


def begin(source, target, sem):
    copy = pltpu.make_async_copy(source, target, sem)
    copy.start()
    return copy


def pack_body(idx_ref, field_hbm, cot_hbm, out_hbm, field_ref, cot_ref, out_ref, sem):
    samples, rows, _, channels = field_ref.shape
    loads, saves = [], []
    for s in range(samples):
        at = s + samples * idx_ref[1]
        loads.append(begin(field_hbm.at[at], field_ref.at[s], sem.at[s]))
        loads.append(begin(cot_hbm.at[at], cot_ref.at[s], sem.at[samples + s]))
    for s in range(samples):
        for i, ref in enumerate((field_ref, cot_ref)):
            loads[2 * s + i].wait()
            for q in range(rows // 2):
                for t in range(channels // 128):
                    span = slice(t * 128, (t + 1) * 128)
                    one, two = ref[s, 2 * q, :, span], ref[s, 2 * q + 1, :, span]
                    left, right = interleave(one.astype(F32), two.astype(F32))
                    out_ref[4 * s + 2 * t, i, q] = left.astype(BF16)
                    out_ref[4 * s + 2 * t + 1, i, q] = right.astype(BF16)
        span = pl.ds(4 * s, 4)
        saves.append(begin(out_ref.at[span], out_hbm.at[span], sem.at[2 * samples + s]))
    for save in saves:
        save.wait()


def unpack_body(in_ref, out_hbm, out_ref, sem):
    samples, rows, _, channels = out_ref.shape
    saves = []
    for s in range(samples):
        for q in range(rows // 2):
            for t in range(channels // 128):
                span = slice(t * 128, (t + 1) * 128)
                one, two = in_ref[4 * s + 2 * t, q], in_ref[4 * s + 2 * t + 1, q]
                one, two = interleave(one.astype(F32), two.astype(F32))
                out_ref[s, 2 * q, :, span] = one.astype(BF16)
                out_ref[s, 2 * q + 1, :, span] = two.astype(BF16)
        saves.append(begin(out_ref.at[s], out_hbm.at[s], sem.at[s]))
    for save in saves:
        save.wait()


def prepare_body(idx_ref, own_hbm, far_hbm, ta_hbm, ts_hbm, w0_ref, w1_ref, ta_ref, ts_ref, sem):
    quarter = w0_ref.shape[1] // 2

    def fetch(source, target, layer):
        copies = []
        for z in range(4):
            at = 4 * quarter * z + quarter * (idx_ref[0] if z < 2 else 3 - idx_ref[0])
            part = target.at[z // 2, pl.ds((z % 2) * quarter, quarter)]
            origin = source.at[0, pl.ds(at, quarter)]
            copies.append(pltpu.make_async_copy(origin, part, sem.at[4 * layer + z]))
        return copies

    tables = [begin(ta_hbm, ta_ref, sem.at[8]), begin(ts_hbm, ts_ref, sem.at[9])]
    front = idx_ref[1] == 0

    @pl.when(front)
    def _():
        for copy in fetch(own_hbm, w0_ref, 0) + fetch(far_hbm, w1_ref, 1):
            copy.start()

    @pl.when(jnp.logical_not(front))
    def _():
        for copy in fetch(far_hbm, w0_ref, 0) + fetch(own_hbm, w1_ref, 1):
            copy.start()

    for copy in fetch(own_hbm, w0_ref, 0) + fetch(own_hbm, w1_ref, 1) + tables:
        copy.wait()


def store_spectrum(q, value, spec_ref):
    spec_ref[pl.ds(q, 128, stride=32), :] = value


def spectrum_at(q, grid_ref):
    return grid_ref[q * 128 : (q + 1) * 128, :].astype(BF16)


def analyse(spec_ref, table_ref, slot_ref, out_ref):
    degrees = table_ref.shape[0] - 1
    pairs = degrees // 2

    low = low_lanes((pairs, 128))

    def order(m):
        rows = spec_ref[m * 2 * pairs : (m + 1) * 2 * pairs, :].astype(BF16)
        return jnp.concatenate([rows[:pairs], rows[pairs:]], axis=1)

    for pos in range(degrees + 1):
        right, left = order(min(degrees - pos, degrees - 1)), table_ref[pos]
        if pos < pairs:
            right = jnp.concatenate([right, order(pos)], axis=0)
        else:
            left = left[:, :pairs]
        both = dot(left, right)
        even, odd = both[:pairs], both[pairs:]
        value = jnp.where(low, even[:, :128], odd[:, 128:]) + turned(
            jnp.where(low, even[:, 128:], odd[:, :128])
        )
        slot_ref[pl.ds(pos, pairs, stride=SLOTS), :] = value
    for pos in range(degrees + 1, SLOTS):
        slot_ref[pl.ds(pos, pairs, stride=SLOTS), :] = jnp.zeros((pairs, 128), F32)
    blocks, rows, _ = out_ref.shape
    for b in range(blocks):
        out_ref[b] = slot_ref[b * rows : (b + 1) * rows, :].astype(BF16)


def synthesise(in_ref, table_ref, slot_ref, grid_ref):
    degrees = table_ref.shape[0]
    pairs = degrees // 2
    blocks, rows, _ = in_ref.shape
    for b in range(blocks):
        slot_ref[b * rows : (b + 1) * rows, :] = in_ref[b].astype(F32)

    for m in range(degrees):
        right = slot_ref[pl.ds(degrees - m, pairs, stride=SLOTS), :]
        left = table_ref[m]
        if m < pairs:
            low = slot_ref[pl.ds(m, pairs, stride=SLOTS), :]
            right = jnp.concatenate([right, low], axis=0)
        else:
            left = left[:, :pairs]
        both = dot(left, right.astype(BF16))
        real, imag = interleave(both[:pairs], both[pairs:])
        grid_ref[pl.ds(2 * m, pairs, stride=2 * degrees), :] = real
        grid_ref[pl.ds(2 * m + 1, pairs, stride=2 * degrees), :] = imag


def gelu_parts(pre):
    cdf = normal_cdf(pre)
    density = jnp.exp(-0.5 * pre * pre) * (1.0 / math.sqrt(2.0 * math.pi))
    return pre * cdf, cdf + pre * density


def beside(first, second):
    return jnp.concatenate([first, second], axis=1)


def spectra_at(d, grid_ref):
    return beside(spectrum_at(2 * d, grid_ref), spectrum_at(2 * d + 1, grid_ref))


def store_spectra(d, value, spec_ref):
    for q in range(2):
        store_spectrum(2 * d + q, value[:, q * 128 : (q + 1) * 128], spec_ref)


def first_body(recv_ref, ana_ref, ta_ref, out_ref, spec_ref, slot_ref):
    basis = ana_ref[...]
    for d in range(recv_ref.shape[0]):
        field = beside(recv_ref[d, 0, 0], recv_ref[d, 0, 1])
        store_spectra(d, dot(basis, field), spec_ref)
    analyse(spec_ref, ta_ref, slot_ref, out_ref)


def layer0_body(in_ref, recv_ref, syn_ref, ana_ref, ts_ref, ta_ref, h_ref, slope_ref, out_ref,
                spec_ref, grid_ref, slot_ref):
    synthesise(in_ref, ts_ref, slot_ref, grid_ref)
    syn, ana = syn_ref[...], ana_ref[...]
    for d in range(recv_ref.shape[0]):
        pre = dot(syn, spectra_at(d, grid_ref))
        made = []
        for q in range(2):
            value, slope = gelu_parts(pre[:, q * 128 : (q + 1) * 128])
            slope_ref[d, q] = slope.astype(BF16)
            h = (recv_ref[d, 0, q].astype(F32) + value).astype(BF16)
            h_ref[d, q] = h
            made.append(h)
        store_spectra(d, dot(ana, beside(*made)), spec_ref)
    analyse(spec_ref, ta_ref, slot_ref, out_ref)


def layer1_body(in_ref, recv_ref, h_ref, syn_ref, ana_ref, ts_ref, ta_ref, top_ref, out_ref,
                spec_ref, grid_ref, slot_ref):
    synthesise(in_ref, ts_ref, slot_ref, grid_ref)
    syn, ana = syn_ref[...], ana_ref[...]
    for d in range(recv_ref.shape[0]):
        pre = dot(syn, spectra_at(d, grid_ref))
        made = []
        for q in range(2):
            value, slope = gelu_parts(pre[:, q * 128 : (q + 1) * 128])
            top_ref[d, q] = (h_ref[d, q].astype(F32) + value).astype(BF16)
            made.append((recv_ref[d, 1, q].astype(F32) * slope).astype(BF16))
        store_spectra(d, dot(ana, beside(*made)), spec_ref)
    analyse(spec_ref, ta_ref, slot_ref, out_ref)


def back1_body(in_ref, recv_ref, slope_ref, syn_ref, ana_ref, ts_ref, ta_ref, g_ref, out_ref,
               spec_ref, grid_ref, slot_ref):
    synthesise(in_ref, ts_ref, slot_ref, grid_ref)
    syn, ana = syn_ref[...], ana_ref[...]
    for d in range(recv_ref.shape[0]):
        back = dot(syn, spectra_at(d, grid_ref))
        made = []
        for q in range(2):
            g = (recv_ref[d, 1, q].astype(F32) + back[:, q * 128 : (q + 1) * 128]).astype(BF16)
            g_ref[d, q] = g
            made.append((g.astype(F32) * slope_ref[d, q].astype(F32)).astype(BF16))
        store_spectra(d, dot(ana, beside(*made)), spec_ref)
    analyse(spec_ref, ta_ref, slot_ref, out_ref)


def back0_body(in_ref, g_ref, top_ref, syn_ref, ts_ref, ends_ref, grid_ref, slot_ref, sem):
    move = begin(top_ref, ends_ref.at[1], sem.at[0])
    synthesise(in_ref, ts_ref, slot_ref, grid_ref)
    syn = syn_ref[...]
    for d in range(g_ref.shape[0]):
        back = dot(syn, spectra_at(d, grid_ref))
        for q in range(2):
            part = back[:, q * 128 : (q + 1) * 128]
            ends_ref[0, d, q] = (g_ref[d, q].astype(F32) + part).astype(BF16)
    move.wait()


def lower_rows(x_at, r):
    index = lax.broadcasted_iota(jnp.int32, (2 * SLOTS, 256), 0)
    pos = jnp.where(index < SLOTS, index, index - SLOTS)
    return pos <= 16 * (r // 4) + r % 4 + 4 * x_at


def mix_body(backward, idx_ref, in_ref, w_ref, out_ref, coef_ref):
    pairs = w_ref.shape[1]
    contract = (((1,), (1 if backward else 0,)), ((), ()))
    rows = 2 * SLOTS
    for rr in range(pairs // 2):
        span = slice(rr * rows, (rr + 1) * rows)
        blocks = [in_ref[b, span].astype(F32) for b in range(4)]
        a0, a1 = interleave(blocks[0], blocks[1])
        b0, b1 = interleave(blocks[2], blocks[3])
        real = jnp.concatenate([a0, b0], axis=1)
        imag = jnp.concatenate([a1, b1], axis=1)
        reals, imags = [], []
        for r in (2 * rr, 2 * rr + 1):
            part = slice((r % 2) * SLOTS, (r % 2 + 1) * SLOTS)
            stack = jnp.concatenate([real[part], imag[part]], axis=0).astype(BF16)
            coef_ref[r] = stack
            one = lax.dot_general(stack, w_ref[0, r], contract, preferred_element_type=F32)
            two = lax.dot_general(
                stack, w_ref[1, pairs - 1 - r], contract, preferred_element_type=F32
            )
            mixed = jnp.where(lower_rows(idx_ref[0], r), one, two)
            reals.append(mixed[:SLOTS])
            imags.append(mixed[SLOTS:])
        real = jnp.concatenate(reals, axis=0)
        imag = jnp.concatenate(imags, axis=0)
        for t in range(2):
            lanes = slice(t * 128, (t + 1) * 128)
            left, right = interleave(real[:, lanes], imag[:, lanes])
            out_ref[2 * t, span] = left.astype(BF16)
            out_ref[2 * t + 1, span] = right.astype(BF16)


def grad_body(idx_ref, coef_ref, grad_ref, out_ref):
    pairs = coef_ref.shape[0]
    over = (((0,), (0,)), ((), ()))
    for r in range(pairs):
        grad = grad_ref[r].astype(F32)
        lower = lower_rows(idx_ref[0], r)
        pieces = (jnp.where(lower, grad, 0.0), jnp.where(lower, 0.0, grad))
        for at, piece in zip((r, 2 * pairs - 1 - r), pieces):
            place = 4 * ((at % 4 + 4 - idx_ref[2]) % 4) + (at // 4 + 4 - idx_ref[3]) % 4
            made = lax.dot_general(
                coef_ref[r], piece.astype(BF16), over, preferred_element_type=F32
            )
            out_ref[place] = made.astype(BF16)


def add_body(layer, idx_ref, first_any, second_any, *rest):
    parts, (first_ref, second_ref, sem) = rest[:4], rest[4:]

    @pl.when(idx_ref[1] == layer)
    def _():
        loads = []
        for k in range(4):
            span = pl.ds(4 * k, 4)
            loads.append(begin(first_any.at[span], first_ref.at[span], sem.at[2 * k]))
            loads.append(begin(second_any.at[span], second_ref.at[span], sem.at[2 * k + 1]))
        for k, part_ref in enumerate(parts):
            loads[2 * k].wait()
            loads[2 * k + 1].wait()
            for i in range(4):
                total = first_ref[4 * k + i].astype(F32) + second_ref[4 * k + i].astype(F32)
                part_ref[i] = total.astype(BF16)


def fold_body(idx_ref, *refs):
    parts = refs[8:]

    def write(first, second, third, fourth):
        for k, part_ref in enumerate(parts):
            total = first[k].astype(F32) + second[k].astype(F32)
            part_ref[0] = (total + third[k].astype(F32) + fourth[k].astype(F32)).astype(BF16)

    @pl.when(idx_ref[1] == 0)
    def _():
        write(*refs[:4])

    @pl.when(idx_ref[1] == 1)
    def _():
        write(*refs[4:8])


def mean_body(count, first, second, third, fourth, out_ref):
    total = first[...].astype(F32) + second[...].astype(F32)
    total += third[...].astype(F32) + fourth[...].astype(F32)
    out_ref[...] = total / count


def local(ta, ts, fields_in, cotangent, weights):
    rows_all, lat_rows, longitudes, channels = fields_in.shape
    degrees = longitudes // 2
    samples = rows_all // 2
    section = lax.axis_index("section")
    x_at, z_at, y_at = lax.axis_index("x"), lax.axis_index("z"), lax.axis_index("dp")
    idx = jnp.stack([x_at, section, y_at, z_at]).astype(jnp.int32)
    syn_np = longitude_table(longitudes, degrees)
    syn = jnp.asarray(syn_np)
    ana = jnp.asarray(np.ascontiguousarray(syn_np.T))
    swap = [(0, 1), (1, 0)]
    pairs = degrees // 2
    q_rows = lat_rows // 2

    vmem = pl.BlockSpec(memory_space=pltpu.VMEM)
    smem = pl.BlockSpec(memory_space=pltpu.SMEM)
    hbm = pl.BlockSpec(memory_space=pltpu.HBM)
    half_shape = (16, q_rows, longitudes, 128)
    half = pltpu.VMEM(half_shape, BF16)
    spec = pltpu.VMEM((4, pairs // 4 * SLOTS, 128), BF16)
    coef = pltpu.VMEM((pairs // 4, 2 * SLOTS, channels), BF16)
    product = pltpu.VMEM((degrees // 4, channels, channels), BF16)
    chosen = pltpu.VMEM((2, pairs // 4, channels, channels), BF16)
    tall = pltpu.VMEM((pairs * 128, 128), F32)
    slots = pltpu.VMEM((pairs * SLOTS, 128), F32)

    def far_away(array):
        return pltpu.with_memory_space_constraint(array, pltpu.HBM)

    def near(array):
        return pltpu.with_memory_space_constraint(array, pltpu.VMEM)

    def call(time, body, ins, shapes, scratches, *args, sems=0, outs=None):
        many = isinstance(shapes, list)
        return pl.pallas_call(
            body,
            in_specs=ins,
            out_specs=outs or ([vmem] * len(shapes) if many else vmem),
            out_shape=shapes,
            scratch_shapes=scratches + [pltpu.SemaphoreType.DMA((sems,))] * (sems > 0),
            cost_estimate=cost(time),
            compiler_params=params(),
        )(*args)

    quarter_field = pltpu.VMEM((samples, lat_rows, longitudes, channels), BF16)
    packed = call(
        3, pack_body, [smem, hbm, hbm], pltpu.HBM((16, 2) + half_shape[1:], BF16),
        [quarter_field] * 2 + [pltpu.VMEM((16, 2) + half_shape[1:], BF16)],
        idx, far_away(fields_in), far_away(cotangent), sems=3 * samples, outs=hbm,
    )
    far = lax.ppermute(weights, "section", swap)
    w0, w1, ta, ts = call(
        2, prepare_body, [smem] + [hbm] * 4,
        [chosen, chosen, pltpu.VMEM(ta.shape, BF16), pltpu.VMEM(ts.shape, BF16)], [],
        idx, far_away(weights), far_away(far), far_away(ta), far_away(ts), sems=10,
    )
    recv = near(lax.all_to_all(packed, ("z", "x"), 0, 0, tiled=True))

    def turn(value):
        return near(lax.all_to_all(value, "x", 0, 0, tiled=True))

    def mix_call(value, weight, backward):
        def body(*refs):
            mix_body(backward, *refs)

        return call(2, body, [smem, vmem, vmem], [spec, coef], [], idx, value, weight)

    row = pltpu.VMEM((4, channels, channels), BF16)
    single = pltpu.VMEM((1, channels, channels), BF16)

    def exchange(parts, axes, routes):
        return [
            part if route is None else near(lax.ppermute(part, axes, route))
            for part, route in zip(parts, routes)
        ]

    def along_dp(first, second, layer):
        made = call(3, grad_body, [smem, vmem, vmem], product, [], idx, first, second)
        got = lax.ppermute(made, "section", [(1 - layer, layer)])
        anywhere = pl.BlockSpec(memory_space=pl.ANY)

        def add(*refs):
            add_body(layer, *refs)

        parts = call(
            2, add, [smem] + [anywhere] * 2, [row] * 4, [product] * 2, idx, made, got, sems=8
        )
        routes = [None]
        for k in range(1, 4):
            routes.append([(4 * layer + i, 4 * layer + (i + k) % 4) for i in range(4)])
        return exchange(parts, ("section", "dp"), routes)

    def together(value, others):
        value, *others = lax.optimization_barrier((value, *others))
        return near(value), [near(other) for other in others]

    value = call(3, first_body, [vmem] * 3, spec, [tall, slots], recv, ana, ta)
    value, coef0 = mix_call(turn(value), w0, False)
    h1, slope, value = call(
        6, layer0_body, [vmem] * 6, [half, half, spec], [tall, tall, slots],
        turn(value), recv, syn, ana, ts, ta,
    )
    value, coef1 = mix_call(turn(value), w1, False)
    top, value = call(
        6, layer1_body, [vmem] * 7, [half, spec], [tall, tall, slots],
        turn(value), recv, h1, syn, ana, ts, ta,
    )
    value, grad1 = mix_call(turn(value), w1, True)
    g1, value = call(
        5, back1_body, [vmem] * 7, [half, spec], [tall, tall, slots],
        turn(value), recv, slope, syn, ana, ts, ta,
    )
    value, grad0 = mix_call(turn(value), w0, True)
    parts1 = along_dp(coef1, grad1, 1)
    grad0, early = together(grad0, [parts1[k] for k in (0, 1, 3)])
    parts1 = [early[0], early[1], parts1[2], early[2]]
    value = turn(value)
    ends = call(
        4, back0_body, [vmem] * 5, pltpu.VMEM((2,) + half_shape, BF16), [tall, slots],
        value, g1, top, syn, ts, sems=1,
    )
    ends = ends.reshape((32,) + half_shape[1:])
    ends = near(lax.all_to_all(ends, ("section", "z", "x"), 0, 0, tiled=True))
    section_ends = call(
        3, unpack_body, [vmem], pltpu.HBM(fields_in.shape, BF16),
        [pltpu.VMEM(fields_in.shape, BF16)], ends, sems=rows_all, outs=hbm,
    )[None]

    across = []
    for k in range(4):
        across.append([])
        for z in range(4):
            for x in range(4):
                there = (z + k) % 4
                across[k].append((4 * z + x, 4 * there + (x if there < 2 else 3 - x)))
    parts0 = along_dp(coef0, grad0, 0)
    parts = call(2, fold_body, [smem] + [vmem] * 8, [single] * 4, [], idx, *parts0, *parts1)
    parts = exchange(parts, ("z", "x"), across)
    batch_count = rows_all * lax.axis_size("dp")

    def mean(*refs):
        mean_body(batch_count, *refs)

    total = call(1, mean, [vmem] * 4, jax.ShapeDtypeStruct(single.shape, F32), [], *parts)
    return (section_ends, total[None])


def solution(mesh):
    grid = Mesh(mesh.devices.reshape(2, 4, 4, 4), ("section", "z", "x", "dp"))
    rows = P("dp", ("z", "x"), None, None)
    in_specs = (rows, rows, P("section", None, None, None))
    out_specs = (
        P("section", "dp", ("z", "x"), None, None),
        P("section", ("z", "x", "dp"), None, None),
    )
    ta, ts = polar_tables(64, 4)

    def body(fields_in, cotangent, weights):
        return local(jnp.asarray(ta), jnp.asarray(ts), fields_in, cotangent, weights)

    return jax.shard_map(body, mesh=grid, in_specs=in_specs, out_specs=out_specs, check_vma=False)
```
